128 devices in a mesh: px: 16 (over y, x), py: 8 (over z, core).
Axes of the slice: x: 4, y: 4, z: 4, core: 2. Of those that a mesh axis runs over, the one named last changes fastest.
Arguments:
- block_vectors: float32 [393216, 256], P(('px', 'py')), may hold values from -6 to 6
- stiff_tiles: float32 [3072, 12, 128, 128], P(('px', 'py')), may hold values from -0.15625 to 0.15625
- col_index: int32 [3072, 12], P(('px', 'py')), may hold values from 0 to 39
- send_lists: int32 [128, 4, 4], P(('px', 'py')), may hold values from 0 to 23
- send_counts: int32 [128, 4], P(('px', 'py')), may hold values from 1 to 4, as said below
- part_blocks: int32 [128], P(('px', 'py')), may hold values from 12 to 24, as said below
Outputs:
- basis: float32 [393216, 256], P(('px', 'py'))
- upper_factor: float32 [256, 256], replicated
The draws below stay inside these ranges and needn't reach their ends.
Inputs may be any that keep to these rules, and one draw needn't show every extreme that they name: `send_counts`: in every draw some partitions send full lists of 4 blocks in some direction. `part_blocks`: in every draw some partitions have all 24 blocks live.
All inputs are finite; a program needn't handle non-finite values.
Results may differ from the reference program's by a relative error of at most 0.000053.
Values sent between devices are 32-bit elements; how exact they have to be, the bound alone decides.
No kernel may reach another device: no remote copies, remote signals or barrier semaphores. Data moves between devices by JAX's collectives and lax.ppermute only.
A program may use at most 192 MiB of HBM per device.

```python
import jax
import jax.numpy as jnp
from jax import lax

BS = 128
K = 256
NBD = 24
TPR = 12
GMAX = 4
NB = 3072
NROWS = 393216
N_PX = 16
N_PY = 8
DEVICES = 128


def draw_send_counts(key, part):
    key = jax.random.fold_in(key, 11)
    values = jax.random.randint(key, (DEVICES, 4), 1, GMAX + 1)
    dev = jnp.arange(DEVICES, dtype=jnp.int32)[:, None]
    direc = jnp.arange(4, dtype=jnp.int32)[None, :]
    full = (dev + direc) % 3 == 0
    return jnp.where(full, GMAX, values).astype(jnp.int32)


def draw_part_blocks(key, part):
    key = jax.random.fold_in(key, 23)
    values = jax.random.randint(key, (DEVICES,), NBD // 2, NBD + 1)
    dev = jnp.arange(DEVICES, dtype=jnp.int32)
    return jnp.where(dev % 5 == 0, NBD, values).astype(jnp.int32)


def place_ends(values, rng, least, top_value):
    index_at = [jax.random.randint(jax.random.fold_in(rng, axis), (), 0, length) for axis, length in enumerate(values.shape)]
    main_axis = values.shape.index(max(values.shape))
    next_to = index_at[:main_axis] + [(index_at[main_axis] + 1) % values.shape[main_axis]] + index_at[main_axis + 1:]
    return values.at[tuple(index_at)].set(least).at[tuple(next_to)].set(top_value)


def level_of(rng, extent, split, least, high):
    factor_of, own = 1.0, jax.random.fold_in(rng, 6)
    for dim, parts in split:
        heights = jnp.exp(jax.random.uniform(jax.random.fold_in(own, dim), (parts,), jnp.float32, least / len(split), high / len(split)))
        factor_of = factor_of * jnp.repeat(heights, extent[dim] // parts).reshape([-1 if axis == dim else 1 for axis in range(len(extent))])
    return factor_of


def gaussian(own_key, shape, spread, reach, split=(), held_as=jnp.bfloat16):
    values = spread * jax.random.normal(own_key, shape, jnp.float32)
    if split:
        values = values * level_of(own_key, shape, split, -0.22, 0.18)
    return jnp.clip(values, -reach, reach).astype(held_as)


def setup_inputs(seed: int = 0) -> dict:
    key_list = jax.random.split(jax.random.key(seed), 7)
    block_vectors = gaussian(key_list[0], (NROWS, K), 1.0, 6.0, ((0, 128),), jnp.float32)
    stiff_tiles = gaussian(key_list[1], (NB, TPR, BS, BS), (TPR * BS) ** -0.5, 0.15625, ((0, 128),), jnp.float32)
    col_index = place_ends(jax.random.randint(key_list[2], (NB, TPR), 0, NBD + 4 * GMAX), jax.random.fold_in(key_list[2], 1), 0, (NBD + 4 * GMAX) - 1).astype(jnp.int32)
    send_lists = place_ends(jax.random.randint(key_list[3], (DEVICES, 4, GMAX), 0, NBD), jax.random.fold_in(key_list[3], 1), 0, NBD - 1).astype(jnp.int32)
    send_counts = draw_send_counts(jax.random.fold_in(key_list[6], 71), 0)
    part_blocks = draw_part_blocks(jax.random.fold_in(key_list[6], 71), 0)
    return dict(block_vectors=block_vectors, stiff_tiles=stiff_tiles, col_index=col_index, send_lists=send_lists, send_counts=send_counts, part_blocks=part_blocks)


def reference(block_vectors, stiff_tiles, col_index, send_lists, send_counts, part_blocks):
    hp = lax.Precision.HIGHEST
    dev = jnp.arange(DEVICES, dtype=jnp.int32)
    prow = dev // N_PY
    pcol = dev % N_PY
    src_p = jnp.stack([prow - 1, prow + 1, prow, prow], axis=1)
    src_q = jnp.stack([pcol, pcol, pcol - 1, pcol + 1], axis=1)
    inside = (src_p >= 0) & (src_p < N_PX) & (src_q >= 0) & (src_q < N_PY)
    source = jnp.clip(src_p, 0, N_PX - 1) * N_PY + jnp.clip(src_q, 0, N_PY - 1)
    direc = jnp.arange(4, dtype=jnp.int32)
    slots = jnp.arange(GMAX, dtype=jnp.int32)
    picked = send_lists[source[:, :, None], direc[None, :, None], slots[None, None, :]]
    ghost_global = (source[:, :, None] * NBD + picked).reshape(DEVICES, 4 * GMAX)
    live = inside[:, :, None] & (slots[None, None, :] < send_counts[source, direc[None, :]][:, :, None])
    ghost_weight = live.reshape(DEVICES, 4 * GMAX).astype(jnp.float32)
    own_global = dev[:, None] * NBD + jnp.arange(NBD, dtype=jnp.int32)[None, :]
    table_global = jnp.concatenate([own_global, ghost_global], axis=1)
    table_weight = jnp.concatenate([jnp.ones((DEVICES, NBD), jnp.float32), ghost_weight], axis=1)
    cols = col_index.reshape(DEVICES, NBD, TPR)
    global_idx = jnp.take_along_axis(table_global, cols.reshape(DEVICES, NBD * TPR), axis=1).reshape(DEVICES, NBD, TPR)
    weights = jnp.take_along_axis(table_weight, cols.reshape(DEVICES, NBD * TPR), axis=1).reshape(DEVICES, NBD, TPR)
    blocks_all = block_vectors.reshape(NB, BS, K)
    tiles = stiff_tiles.reshape(DEVICES, NBD, TPR, BS, BS)
    keep = (jnp.arange(NBD, dtype=jnp.int32)[None, :] < part_blocks[:, None]).astype(jnp.float32)

    def one_part(item):
        tile_dev, idx_dev, w_dev, keep_dev = item
        operand = blocks_all[idx_dev] * w_dev[:, :, None, None]
        out = jnp.einsum('btij,btjk->bik', tile_dev, operand, precision=hp)
        return out * keep_dev[:, None, None]
    applied = lax.map(one_part, (tiles, global_idx, weights, keep)).reshape(NROWS, K)
    gram = jnp.dot(applied.T.astype(jnp.float32), applied.astype(jnp.float32), precision=hp, preferred_element_type=jnp.float32) / NROWS
    lower = jnp.linalg.cholesky(gram)
    inverse_lower = lax.linalg.triangular_solve(lower, jnp.eye(K, dtype=jnp.float32), left_side=True, lower=True)
    inverse_upper = inverse_lower.T
    basis = jnp.dot(applied.astype(jnp.float32), inverse_upper.astype(jnp.float32), precision=hp, preferred_element_type=jnp.float32)
    return (basis, lower.T)
```

```python
import functools
import itertools

import jax
import jax.numpy as jnp
from jax import lax
from jax.experimental import pallas as pl
from jax.experimental.pallas import tpu as pltpu
from jax.sharding import PartitionSpec as P

AXES = ("px", "py")
SIDE = 4
BS = 128
K = 256
NBD = 24
TPR = 12
GMAX = 4
NROWS = 393216
HALF = 136
F32 = jnp.float32
BF16 = jnp.bfloat16
MB = 1 << 20


def device_at(x, y, z, core):
    return (y * SIDE + x) * 8 + z * 2 + core


def route(move):
    places = itertools.product(range(SIDE), range(SIDE), range(SIDE), range(2))
    return [(device_at(*p), device_at(*move(*p))) for p in places]


def pair_route(dim, odd):
    def move(x, y, z, core):
        at = [x, y, z]
        v = at[dim]
        if odd:
            at[dim] = (v - 1) % SIDE if v % 2 == 0 else (v + 1) % SIDE
        else:
            at[dim] = v ^ 1
        return (*at, core)

    return route(move)


CORE_ROUTE = route(lambda x, y, z, core: (x, y, z, 1 - core))


def shifted(block, axis, distance):
    devices = range(lax.axis_size(axis))
    pairs = [(i - distance, i) for i in devices if i - distance in devices]
    return lax.ppermute(block, axis, pairs)


def sum_everywhere(packed):
    core = lax.axis_index("py") % 2
    mine = lax.dynamic_slice_in_dim(packed, core * HALF, HALF, 0)
    other = lax.dynamic_slice_in_dim(packed, (1 - core) * HALF, HALF, 0)
    total = mine + lax.ppermute(other, AXES, CORE_ROUTE)
    for dim in range(3):
        for odd in (False, True):
            total = total + lax.ppermute(total, AXES, pair_route(dim, odd))
    theirs = lax.ppermute(total, AXES, CORE_ROUTE)
    low = jnp.where(core == 0, total, theirs)
    high = jnp.where(core == 0, theirs, total)
    return low, high


def pack_kernel(lists, counts, own, *refs):
    outs, zero, sems = refs[:4], refs[4], refs[5]
    zero[...] = jnp.zeros_like(zero)
    for e in range(4):
        for s in range(GMAX):
            block = lists[e * GMAX + s]

            @pl.when(s < counts[e])
            def _():
                pltpu.make_async_copy(own.at[block], outs[e].at[s], sems.at[e, s]).start()

            @pl.when(s >= counts[e])
            def _():
                pltpu.make_async_copy(zero, outs[e].at[s], sems.at[e, s]).start()

    for e in range(4):
        for s in range(GMAX):
            pltpu.make_async_copy(zero, outs[e].at[s], sems.at[e, s]).wait()


def pack_ghosts(own_blocks, lists, counts):
    smem = pl.BlockSpec(memory_space=pltpu.SMEM)
    anywhere = pl.BlockSpec(memory_space=pl.ANY)
    out = jax.ShapeDtypeStruct((GMAX, BS, K), F32)
    return pl.pallas_call(
        pack_kernel,
        out_shape=[out] * 4,
        in_specs=[smem, smem, anywhere],
        out_specs=[anywhere] * 4,
        scratch_shapes=[pltpu.VMEM((BS, K), F32), pltpu.SemaphoreType.DMA((4, GMAX))],
        cost_estimate=pl.CostEstimate(flops=0, bytes_accessed=4 * MB, transcendentals=0),
        name="pack_ghosts",
    )(lists, counts, own_blocks)


def split(x):
    high = x.astype(BF16)
    return high, (x - high.astype(F32)).astype(BF16)


def dot(a, b):
    return lax.dot_general(a, b, (((1,), (0,)), ((), ())), preferred_element_type=F32)


def gather_row(cols, row, tile_list, col_list, low, high, zero_block):
    n = jnp.int32(0)
    for t in range(TPR):
        c = cols[row * TPR + t]
        tile_list[n] = t
        col_list[n] = c - low
        n = n + jnp.where((c >= low) & (c < high), 1, 0)
    tile_list[n] = 0
    col_list[n] = zero_block
    return (n + 1) // 2


def add_pairs(pairs, tile_list, col_list, tiles, xh, xl, acc):
    def pair(p, _):
        t0, t1 = tile_list[2 * p], tile_list[2 * p + 1]
        c0, c1 = col_list[2 * p], col_list[2 * p + 1]
        th, tl = split(jnp.concatenate([tiles[0, t0], tiles[0, t1]], axis=1))
        r0 = pl.ds(pl.multiple_of(c0 * BS, BS), BS)
        r1 = pl.ds(pl.multiple_of(c1 * BS, BS), BS)
        bh = jnp.concatenate([xh[r0], xh[r1]], axis=0)
        bl = jnp.concatenate([xl[r0], xl[r1]], axis=0)
        acc[...] += dot(th, bh) + dot(tl, bh) + dot(th, bl)
        return 0

    lax.fori_loop(0, pairs, pair, 0)


def own_kernel(cols, live, own, tiles, out, xh, xl, acc, tile_list, col_list):
    row = pl.program_id(0)

    @pl.when(row == 0)
    def _():
        xh[NBD * BS :] = jnp.zeros((BS, K), BF16)
        xl[NBD * BS :] = jnp.zeros((BS, K), BF16)

        def convert(b, _):
            rows = pl.ds(pl.multiple_of(b * BS, BS), BS)
            xh[rows], xl[rows] = split(own[rows])
            return 0

        lax.fori_loop(0, NBD, convert, 0)

    acc[...] = jnp.zeros_like(acc)

    @pl.when(row < live[0])
    def _():
        pairs = gather_row(cols, row, tile_list, col_list, 0, NBD, NBD)
        add_pairs(pairs, tile_list, col_list, tiles, xh, xl, acc)

    out[...] = acc[...]


def apply_own(own, tiles, cols, live):
    smem = pl.BlockSpec(memory_space=pltpu.SMEM)
    return pl.pallas_call(
        own_kernel,
        grid=(NBD,),
        out_shape=jax.ShapeDtypeStruct((NBD * BS, K), F32),
        in_specs=[
            smem,
            smem,
            pl.BlockSpec((NBD * BS, K), lambda b: (0, 0)),
            pl.BlockSpec((1, TPR, BS, BS), lambda b: (b, 0, 0, 0)),
        ],
        out_specs=pl.BlockSpec((BS, K), lambda b: (b, 0)),
        scratch_shapes=[
            pltpu.VMEM(((NBD + 1) * BS, K), BF16),
            pltpu.VMEM(((NBD + 1) * BS, K), BF16),
            pltpu.VMEM((BS, K), F32),
            pltpu.SMEM((TPR + 4,), jnp.int32),
            pltpu.SMEM((TPR + 4,), jnp.int32),
        ],
        compiler_params=pltpu.CompilerParams(vmem_limit_bytes=40 * MB),
        cost_estimate=pl.CostEstimate(flops=4 * 10**9, bytes_accessed=25 * MB, transcendentals=0),
        name="apply_own",
    )(cols, live, own, tiles)


def gram_pack(high, low):
    tn = lambda a, b: lax.dot_general(a, b, (((0,), (0,)), ((), ())), preferred_element_type=F32)
    main = tn(high, high)
    cross = tn(high, low)
    gram = main + cross + cross.T
    i = lax.broadcasted_iota(jnp.int32, (BS, BS), 0)
    j = lax.broadcasted_iota(jnp.int32, (BS, BS), 1)
    first, second = gram[:BS, :BS], gram[BS:, BS:]
    diagonal = jnp.sum(jnp.where(i == j, second, 0.0), axis=0, keepdims=True)
    tail = jnp.broadcast_to(diagonal, (2 * HALF - 2 * BS, BS))
    return jnp.concatenate([jnp.where(i <= j, first, second), gram[:BS, BS:], tail], axis=0)


def ghost_kernel(cols, live, part, g0, g1, g2, g3, tiles, out, gram, xh, xl, ah, al, acc, tile_list, col_list):
    row = pl.program_id(0)

    @pl.when(row == 0)
    def _():
        xh[4 * GMAX * BS :] = jnp.zeros((BS, K), BF16)
        xl[4 * GMAX * BS :] = jnp.zeros((BS, K), BF16)
        for e, g in enumerate((g0, g1, g2, g3)):
            for s in range(GMAX):
                rows = pl.ds((e * GMAX + s) * BS, BS)
                xh[rows], xl[rows] = split(g[s])

    acc[...] = part[...]

    @pl.when(row < live[0])
    def _():
        pairs = gather_row(cols, row, tile_list, col_list, NBD, NBD + 4 * GMAX, 4 * GMAX)
        add_pairs(pairs, tile_list, col_list, tiles, xh, xl, acc)

    total = acc[...]
    out[...] = total
    rows = pl.ds(pl.multiple_of(row * BS, BS), BS)
    ah[rows], al[rows] = split(total)

    @pl.when(row == NBD - 1)
    def _():
        gram[...] = gram_pack(ah[...], al[...])


def apply_ghosts(part, ghosts, tiles, cols, live):
    smem = pl.BlockSpec(memory_space=pltpu.SMEM)
    whole = pl.BlockSpec((GMAX, BS, K), lambda b: (0, 0, 0))
    return pl.pallas_call(
        ghost_kernel,
        grid=(NBD,),
        out_shape=[
            jax.ShapeDtypeStruct((NBD * BS, K), F32),
            jax.ShapeDtypeStruct((2 * HALF, BS), F32),
        ],
        in_specs=[smem, smem, pl.BlockSpec((BS, K), lambda b: (b, 0))]
        + [whole] * 4
        + [pl.BlockSpec((1, TPR, BS, BS), lambda b: (b, 0, 0, 0))],
        out_specs=[
            pl.BlockSpec((BS, K), lambda b: (b, 0)),
            pl.BlockSpec((2 * HALF, BS), lambda b: (0, 0)),
        ],
        scratch_shapes=[
            pltpu.VMEM(((4 * GMAX + 1) * BS, K), BF16),
            pltpu.VMEM(((4 * GMAX + 1) * BS, K), BF16),
            pltpu.VMEM((NBD * BS, K), BF16),
            pltpu.VMEM((NBD * BS, K), BF16),
            pltpu.VMEM((BS, K), F32),
            pltpu.SMEM((TPR + 4,), jnp.int32),
            pltpu.SMEM((TPR + 4,), jnp.int32),
        ],
        compiler_params=pltpu.CompilerParams(vmem_limit_bytes=40 * MB),
        cost_estimate=pl.CostEstimate(flops=4 * 10**9, bytes_accessed=25 * MB, transcendentals=0),
        name="apply_ghosts",
    )(cols, live, part, *ghosts, tiles)


def exact(a, b, ca=1, cb=0):
    return lax.dot_general(
        a, b, (((ca,), (cb,)), ((), ())), precision=lax.Precision.HIGHEST, preferred_element_type=F32
    )


def eliminate(square):
    n = square.shape[0]
    i = lax.broadcasted_iota(jnp.int32, (n, n), 0)
    j = lax.broadcasted_iota(jnp.int32, (n, n), 1)
    unit = jnp.where(i == j, 1.0, 0.0).astype(F32)
    groups = n // 8
    left = [square[8 * g : 8 * g + 8] for g in range(groups)]
    right = [unit[8 * g : 8 * g + 8] for g in range(groups)]
    place = lax.broadcasted_iota(jnp.int32, (8, n), 0)
    for p in range(n):
        at, sub = divmod(p, 8)
        row = left[at][sub : sub + 1]
        row_right = right[at][sub : sub + 1]
        inverse = 1.0 / row[:, p : p + 1]
        for g in range(at, groups):
            if g == at and sub == 7:
                continue
            factor = left[g][:, p : p + 1] * inverse
            if g == at:
                factor = jnp.where(place > sub, factor, 0.0)
            left[g] = left[g] - factor * row
            right[g] = right[g] - factor * row_right
    upper = jnp.concatenate(left, axis=0)
    lower = jnp.concatenate(right, axis=0)
    pivot = jnp.sum(jnp.where(i == j, upper, 0.0), axis=1, keepdims=True)
    scale = lax.rsqrt(pivot)
    return jnp.where(i <= j, upper * scale, 0.0), jnp.where(i >= j, lower * scale, 0.0)


def factor(low, high):
    packed = jnp.concatenate([low, high], axis=0) * (1.0 / NROWS)
    mixed, corner, tail = packed[:BS], packed[BS : 2 * BS], packed[2 * BS : 2 * BS + 1]
    i = lax.broadcasted_iota(jnp.int32, (BS, BS), 0)
    j = lax.broadcasted_iota(jnp.int32, (BS, BS), 1)
    turned = mixed.T
    first = jnp.where(i <= j, mixed, turned)
    second = jnp.where(i > j, mixed, jnp.where(i < j, turned, tail))
    r11, x11 = eliminate(first)
    r12 = exact(x11, corner)
    r22, x22 = eliminate(second - exact(r12, r12, 0, 0))
    x21 = -exact(x22, exact(r12, x11, 0, 0))
    zero = jnp.zeros((BS, BS), F32)
    upper = jnp.concatenate(
        [jnp.concatenate([r11, r12], axis=1), jnp.concatenate([zero, r22], axis=1)], axis=0
    )
    lower = jnp.concatenate(
        [jnp.concatenate([x11, zero], axis=1), jnp.concatenate([x21, x22], axis=1)], axis=0
    )
    return upper, lower


def basis_kernel(low, high, applied, basis, upper, wh, wl):
    @pl.when(pl.program_id(0) == 0)
    def _():
        r, x = factor(low[...], high[...])
        upper[...] = r
        wh[...], wl[...] = split(x.T)

    ah, al = split(applied[...])
    basis[...] = dot(ah, wh[...]) + dot(al, wh[...]) + dot(ah, wl[...])


def orthonormalize(low, high, applied):
    rows = 512
    half = pl.BlockSpec((HALF, BS), lambda b: (0, 0))
    return pl.pallas_call(
        basis_kernel,
        grid=(NBD * BS // rows,),
        out_shape=[
            jax.ShapeDtypeStruct((NBD * BS, K), F32),
            jax.ShapeDtypeStruct((K, K), F32),
        ],
        in_specs=[half, half, pl.BlockSpec((rows, K), lambda b: (b, 0))],
        out_specs=[
            pl.BlockSpec((rows, K), lambda b: (b, 0)),
            pl.BlockSpec((K, K), lambda b: (0, 0)),
        ],
        scratch_shapes=[pltpu.VMEM((K, K), BF16), pltpu.VMEM((K, K), BF16)],
        compiler_params=pltpu.CompilerParams(vmem_limit_bytes=40 * MB),
        cost_estimate=pl.CostEstimate(flops=10**9, bytes_accessed=7 * MB, transcendentals=0),
        name="factor_and_basis",
    )(low, high, applied)


def body(block_vectors, stiff_tiles, col_index, send_lists, send_counts, part_blocks):
    own_blocks = block_vectors.reshape(NBD, BS, K)
    cols = col_index.reshape(NBD * TPR)
    packed = pack_ghosts(own_blocks, send_lists.reshape(4 * GMAX), send_counts.reshape(4))
    ghosts = [
        shifted(packed[0], "px", 1),
        shifted(packed[1], "px", -1),
        shifted(packed[2], "py", 1),
        shifted(packed[3], "py", -1),
    ]
    part = apply_own(block_vectors, stiff_tiles, cols, part_blocks)
    applied, gram = apply_ghosts(part, ghosts, stiff_tiles, cols, part_blocks)
    low, high = sum_everywhere(gram)
    return tuple(orthonormalize(low, high, applied))


def solution(mesh):
    placed = (
        P(AXES, None),
        P(AXES, None, None, None),
        P(AXES, None),
        P(AXES, None, None),
        P(AXES, None),
        P(AXES),
    )
    return jax.shard_map(body, mesh=mesh, in_specs=placed, out_specs=(P(AXES, None), P()), check_vma=False)
```

```python
import functools
import itertools

import jax
import jax.numpy as jnp
from jax import lax
from jax.experimental import pallas as pl
from jax.experimental.pallas import tpu as pltpu
from jax.sharding import PartitionSpec as P

AXES = ("px", "py")
SIDE = 4
BS = 128
K = 256
NBD = 24
TPR = 12
GMAX = 4
NROWS = 393216
HALF = 136
F32 = jnp.float32
BF16 = jnp.bfloat16
MB = 1 << 20
CHUNK = 4
AHEAD = 4
NEAR = 2
STORE = 512


def device_at(x, y, z, core):
    return (y * SIDE + x) * 8 + z * 2 + core


def route(move):
    places = itertools.product(range(SIDE), range(SIDE), range(SIDE), range(2))
    return [(device_at(*p), device_at(*move(*p))) for p in places]


def pair_route(dim, odd):
    def move(x, y, z, core):
        at = [x, y, z]
        v = at[dim]
        if odd:
            at[dim] = (v - 1) % SIDE if v % 2 == 0 else (v + 1) % SIDE
        else:
            at[dim] = v ^ 1
        return (*at, core)

    return route(move)


CORE_ROUTE = route(lambda x, y, z, core: (x, y, z, 1 - core))


def shifted(block, axis, distance):
    devices = range(lax.axis_size(axis))
    pairs = [(i - distance, i) for i in devices if i - distance in devices]
    return lax.ppermute(block, axis, pairs)


def sum_everywhere(packed):
    core = lax.axis_index("py") % 2
    mine = lax.dynamic_slice_in_dim(packed, core * HALF, HALF, 0)
    other = lax.dynamic_slice_in_dim(packed, (1 - core) * HALF, HALF, 0)
    total = mine + lax.ppermute(other, AXES, CORE_ROUTE)
    for dim in range(3):
        for odd in (False, True):
            total = total + lax.ppermute(total, AXES, pair_route(dim, odd))
    theirs = lax.ppermute(total, AXES, CORE_ROUTE)
    low = jnp.where(core == 0, total, theirs)
    high = jnp.where(core == 0, theirs, total)
    return low, high


def on_vmem(x):
    return pltpu.with_memory_space_constraint(x, pltpu.VMEM)


def pack_kernel(lists, counts, own, *refs):
    outs, sems = refs[:4], refs[4]

    def copy(e, s, block):
        return pltpu.make_async_copy(own.at[block], outs[e].at[s], sems.at[e, s])

    for e in range(4):
        for s in range(GMAX):
            alive = s < counts[e]

            @pl.when(alive)
            def _():
                copy(e, s, lists[e * GMAX + s]).start()

            @pl.when(jnp.logical_not(alive))
            def _():
                outs[e][s] = jnp.zeros((BS, K), F32)

    for e in range(4):
        for s in range(GMAX):

            @pl.when(s < counts[e])
            def _():
                copy(e, s, 0).wait()


def pack_ghosts(own_blocks, lists, counts):
    smem = pl.BlockSpec(memory_space=pltpu.SMEM)
    vmem = pl.BlockSpec(memory_space=pltpu.VMEM)
    return pl.pallas_call(
        pack_kernel,
        out_shape=[pltpu.VMEM((GMAX, BS, K), F32)] * 4,
        in_specs=[smem, smem, pl.BlockSpec(memory_space=pltpu.HBM)],
        out_specs=[vmem] * 4,
        scratch_shapes=[pltpu.SemaphoreType.DMA((4, GMAX))],
        compiler_params=pltpu.CompilerParams(vmem_limit_bytes=4 * MB),
        cost_estimate=pl.CostEstimate(flops=0, bytes_accessed=4 * MB, transcendentals=0),
        name="pack_ghosts",
    )(lists, counts, own_blocks)


def split(x):
    high = x.astype(BF16)
    return high, (x - high.astype(F32)).astype(BF16)


def dot(a, b):
    return lax.dot_general(a, b, (((1,), (0,)), ((), ())), preferred_element_type=F32)


def pair_lists(cols, live, own_list, ghost_list):
    def row_pairs(row, counts):
        starts = counts
        for t in range(TPR):
            c = cols[row * TPR + t]
            ghost = jnp.where(c >= NBD, 1, 0)
            for (tile, block, _, _), n, first, mine in (
                (own_list, counts[0], 0, 1 - ghost),
                (ghost_list, counts[1], NBD, ghost),
            ):
                tile[n] = row * TPR + t
                block[n] = c - first
            counts = (counts[0] + 1 - ghost, counts[1] + ghost)
        ends = []
        for (tile, block, rows, _), n, start, zero in (
            (own_list, counts[0], starts[0], NBD),
            (ghost_list, counts[1], starts[1], 4 * GMAX),
        ):
            tile[n] = 0
            block[n] = zero
            end = n + (n & 1)
            for k in range(TPR // 2):
                rows[start // 2 + k] = row
            ends.append(end)
        return tuple(ends)

    zero = jnp.int32(0)
    own_n, ghost_n = lax.fori_loop(0, live[0], row_pairs, (zero, zero))
    for (tile, block, rows, count), n, blank in (
        (own_list, own_n, NBD),
        (ghost_list, ghost_n, 4 * GMAX),
    ):
        for k in range(2 * CHUNK):
            tile[n + k] = 0
            block[n + k] = blank
        for k in range(CHUNK):
            rows[n // 2 + k] = 0
        count[0] = n // 2


def add_chunk(start, lists, tiles, xh, xl, acc):
    tile, block, rows, _ = lists
    for k in range(CHUNK):
        p = start + k
        t0, t1, c0, c1 = tile[2 * p], tile[2 * p + 1], block[2 * p], block[2 * p + 1]
        th, tl = split(jnp.concatenate([tiles[t0], tiles[t1]], axis=1))
        r0 = pl.ds(pl.multiple_of(c0 * BS, BS), BS)
        r1 = pl.ds(pl.multiple_of(c1 * BS, BS), BS)
        bh = jnp.concatenate([xh[r0], xh[r1]], axis=0)
        bl = jnp.concatenate([xl[r0], xl[r1]], axis=0)
        at = pl.ds(pl.multiple_of(rows[p] * BS, BS), BS)
        acc[at] += dot(th, bh) + dot(tl, bh) + dot(th, bl)


def own_kernel(cols, live, own, tiles, part, held, gt, gb, gr, gn, xv, xh, xl, ot, ob, orow, on, xsem, tsem):
    x_copies = [
        pltpu.make_async_copy(own.at[pl.ds(i * BS * 6, BS * 6)], xv.at[pl.ds(i * BS * 6, BS * 6)], xsem.at[i])
        for i in range(4)
    ]

    def fetch(row):
        rows = pl.ds(row * TPR, TPR)
        return pltpu.make_async_copy(tiles.at[rows], held.at[rows], tsem.at[row])

    for c in x_copies:
        c.start()
    for row in range(AHEAD):
        fetch(row).start()
    own_list, ghost_list = (ot, ob, orow, on), (gt, gb, gr, gn)
    pair_lists(cols, live, own_list, ghost_list)
    part[...] = jnp.zeros_like(part)
    xh[NBD * BS :] = jnp.zeros((BS, K), BF16)
    xl[NBD * BS :] = jnp.zeros((BS, K), BF16)
    for i, c in enumerate(x_copies):
        c.wait()

        def convert(b, _):
            rows = pl.ds(pl.multiple_of((i * 6 + b) * BS, BS), BS)
            xh[rows], xl[rows] = split(xv[rows])
            return 0

        lax.fori_loop(0, 6, convert, 0)

    def arrive(row, _):
        fetch(row).wait()

        @pl.when(row + AHEAD < NBD)
        def _():
            fetch(row + AHEAD).start()

        return 0

    pairs = on[0]

    def chunk(i, ready):
        last = jnp.minimum(i * CHUNK + CHUNK, pairs) - 1
        need = jnp.maximum(orow[last] + 1, ready)
        lax.fori_loop(ready, need, arrive, 0)
        add_chunk(i * CHUNK, own_list, held, xh, xl, part)
        return need

    ready = lax.fori_loop(0, (pairs + CHUNK - 1) // CHUNK, chunk, jnp.int32(0))
    lax.fori_loop(ready, NBD, arrive, 0)


def list_shapes(kind):
    return [
        kind((NBD * (TPR + 2) + 4 * CHUNK,), jnp.int32),
        kind((NBD * (TPR + 2) + 4 * CHUNK,), jnp.int32),
        kind((NBD * (TPR + 2) // 2 + 4 * CHUNK,), jnp.int32),
        kind((1,), jnp.int32),
    ]


def apply_own(own, tiles, cols, live):
    smem = pl.BlockSpec(memory_space=pltpu.SMEM)
    vmem = pl.BlockSpec(memory_space=pltpu.VMEM)
    hbm = pl.BlockSpec(memory_space=pltpu.HBM)
    return pl.pallas_call(
        own_kernel,
        out_shape=[
            pltpu.VMEM((NBD * BS, K), F32),
            pltpu.VMEM((NBD * TPR, BS, BS), F32),
            *list_shapes(jax.ShapeDtypeStruct),
        ],
        in_specs=[smem, smem, hbm, hbm],
        out_specs=[vmem, vmem] + [smem] * 4,
        scratch_shapes=[
            pltpu.VMEM((NBD * BS, K), F32),
            pltpu.VMEM(((NBD + 1) * BS, K), BF16),
            pltpu.VMEM(((NBD + 1) * BS, K), BF16),
            *list_shapes(pltpu.SMEM),
            pltpu.SemaphoreType.DMA((4,)),
            pltpu.SemaphoreType.DMA((NBD,)),
        ],
        compiler_params=pltpu.CompilerParams(vmem_limit_bytes=12 * MB),
        cost_estimate=pl.CostEstimate(flops=4 * 10**9, bytes_accessed=25 * MB, transcendentals=0),
        name="apply_own",
    )(cols, live, own, tiles)


def gram_pack(high, low):
    tn = lambda a, b: lax.dot_general(a, b, (((0,), (0,)), ((), ())), preferred_element_type=F32)
    main = tn(high, high)
    cross = tn(high, low)
    gram = main + cross + cross.T
    i = lax.broadcasted_iota(jnp.int32, (BS, BS), 0)
    j = lax.broadcasted_iota(jnp.int32, (BS, BS), 1)
    first, second = gram[:BS, :BS], gram[BS:, BS:]
    diagonal = jnp.sum(jnp.where(i == j, second, 0.0), axis=0, keepdims=True)
    tail = jnp.broadcast_to(diagonal, (2 * HALF - 2 * BS, BS))
    return jnp.concatenate([jnp.where(i <= j, first, second), gram[:BS, BS:], tail], axis=0)


def ghost_kernel(gt, gb, gr, gn, part, held, g0, g1, g2, g3, total, ah, al, gram, xh, xl):
    xh[4 * GMAX * BS :] = jnp.zeros((BS, K), BF16)
    xl[4 * GMAX * BS :] = jnp.zeros((BS, K), BF16)
    for e, g in enumerate((g0, g1, g2, g3)):

        def convert(s, _):
            rows = pl.ds(pl.multiple_of((e * GMAX + s) * BS, BS), BS)
            xh[rows], xl[rows] = split(g[s])
            return 0

        lax.fori_loop(0, GMAX, convert, 0)

    def chunk(i, _):
        add_chunk(i * CHUNK, (gt, gb, gr, gn), held, xh, xl, total)
        return 0

    lax.fori_loop(0, (gn[0] + CHUNK - 1) // CHUNK, chunk, 0)

    def finish(row, _):
        rows = pl.ds(pl.multiple_of(row * BS, BS), BS)
        ah[rows], al[rows] = split(total[rows])
        return 0

    lax.fori_loop(0, NBD, finish, 0)
    gram[...] = gram_pack(ah[...], al[...])


def apply_ghosts(part, held, lists, ghosts):
    smem = pl.BlockSpec(memory_space=pltpu.SMEM)
    vmem = pl.BlockSpec(memory_space=pltpu.VMEM)
    _, ah, al, gram = pl.pallas_call(
        ghost_kernel,
        out_shape=[
            pltpu.VMEM((NBD * BS, K), F32),
            pltpu.VMEM((NBD * BS, K), BF16),
            pltpu.VMEM((NBD * BS, K), BF16),
            jax.ShapeDtypeStruct((2 * HALF, BS), F32),
        ],
        in_specs=[smem] * 4 + [vmem] * 6,
        out_specs=[vmem] * 4,
        scratch_shapes=[
            pltpu.VMEM(((4 * GMAX + 1) * BS, K), BF16),
            pltpu.VMEM(((4 * GMAX + 1) * BS, K), BF16),
        ],
        input_output_aliases={4: 0},
        compiler_params=pltpu.CompilerParams(vmem_limit_bytes=16 * MB),
        cost_estimate=pl.CostEstimate(flops=3 * 10**9, bytes_accessed=25 * MB, transcendentals=0),
        name="apply_ghosts",
    )(*lists, on_vmem(part), on_vmem(held), *[on_vmem(g) for g in ghosts])
    return ah, al, gram


def exact(a, b, ca=1, cb=0):
    return lax.dot_general(
        a, b, (((ca,), (cb,)), ((), ())), precision=lax.Precision.HIGHEST, preferred_element_type=F32
    )


def spread(x):
    return jnp.broadcast_to(x, (8, BS))


def tree_sum(terms):
    while len(terms) > 1:
        pairs = [terms[i] + terms[i + 1] for i in range(0, len(terms) - 1, 2)]
        terms = pairs + terms[len(terms) - len(terms) % 2 :]
    return terms[0]


def eliminate(columns):
    groups, wide = BS // 8, range(len(columns))
    state = [[c[8 * g : 8 * g + 8] for c in columns] for g in range(groups)]
    outs = [[] for _ in columns]
    place = lax.broadcasted_iota(jnp.int32, (8, BS), 0)
    for at in range(groups):
        near = range(at + 1, min(groups, at + 1 + NEAR))
        first = {g: [spread(state[g][0][:, 8 * at + k : 8 * at + k + 1]) for k in range(8)] for g in (at, *near)}
        a = {(i, j): spread(first[at][j][i : i + 1]) for i in range(8) for j in range(i, 8)}
        w = [[spread(state[at][c][k : k + 1]) for c in wide] for k in range(8)]
        inverse, lower = [], {}
        for k in range(8):
            inverse.append(1.0 / a[k, k])
            for i in range(k + 1, 8):
                m = lower[i, k] = a[k, i] * inverse[k]
                for j in range(i, 8):
                    a[i, j] = a[i, j] - m * a[k, j]
                for c in wide:
                    w[i][c] = w[i][c] - m * w[k][c]
        for k in range(8):
            scale = lax.rsqrt(a[k, k])
            for c in wide:
                outs[c].append((w[k][c] * scale)[:1])
        if at + 1 == groups:
            break
        q = [[w[k][c] * inverse[k] for c in wide] for k in range(8)]
        for k in range(6, -1, -1):
            for m in range(k + 1, 8):
                for c in wide:
                    q[k][c] = q[k][c] - lower[m, k] * q[m][c]
        for g in near:
            for c in wide:
                state[g][c] = state[g][c] - tree_sum([first[g][k] * q[k][c] for k in range(8)])
        far = at + 1 + NEAR
        if far < groups:
            rows = []
            for c in wide:
                block = q[0][c]
                for k in range(1, 8):
                    block = jnp.where(place == k, q[k][c], block)
                rows.append(block)
            parts = [jnp.concatenate(rows, axis=1)]
            if at:
                parts.insert(0, jnp.zeros((8 * at, BS * len(columns)), F32))
            parts.append(jnp.zeros((BS - 8 * at - 8, BS * len(columns)), F32))
            update = exact(
                jnp.concatenate([state[g][0] for g in range(far, groups)], axis=0),
                jnp.concatenate(parts, axis=0),
            )
            for n, g in enumerate(range(far, groups)):
                for c in wide:
                    state[g][c] = state[g][c] - update[8 * n : 8 * n + 8, c * BS : c * BS + BS]
    return [jnp.concatenate(rows, axis=0) for rows in outs]


def factor(low, high):
    packed = jnp.concatenate([low, high], axis=0) * (1.0 / NROWS)
    mixed, corner, tail = packed[:BS], packed[BS : 2 * BS], packed[2 * BS : 2 * BS + 1]
    i = lax.broadcasted_iota(jnp.int32, (BS, BS), 0)
    j = lax.broadcasted_iota(jnp.int32, (BS, BS), 1)
    unit = jnp.where(i == j, 1.0, 0.0).astype(F32)
    turned = mixed.T
    first = jnp.where(i <= j, mixed, turned)
    second = jnp.where(i > j, mixed, jnp.where(i < j, turned, tail))
    r11, r12, x11 = eliminate([first, corner, unit])
    x11 = jnp.where(i >= j, x11, 0.0)
    r22, x22 = eliminate([second - exact(r12, r12, 0, 0), unit])
    x22 = jnp.where(i >= j, x22, 0.0)
    x21 = -exact(x22, exact(r12, x11, 0, 0))
    r11, r22 = jnp.where(i <= j, r11, 0.0), jnp.where(i <= j, r22, 0.0)
    zero = jnp.zeros((BS, BS), F32)
    upper = jnp.concatenate(
        [jnp.concatenate([r11, r12], axis=1), jnp.concatenate([zero, r22], axis=1)], axis=0
    )
    lower = jnp.concatenate(
        [jnp.concatenate([x11, zero], axis=1), jnp.concatenate([x21, x22], axis=1)], axis=0
    )
    return upper, lower


def basis_kernel(low, high, ah, al, basis, upper, wh, wl, staged, sems):
    r, x = factor(low[...], high[...])
    upper[...] = r
    wh[...], wl[...] = split(x.T)

    def store(n):
        rows = pl.ds(pl.multiple_of(n * STORE, STORE), STORE)
        return pltpu.make_async_copy(staged.at[rows], basis.at[rows], sems.at[n])

    def chunk(n, _):
        rows = pl.ds(pl.multiple_of(n * STORE, STORE), STORE)
        h, l = ah[rows], al[rows]
        staged[rows] = dot(h, wh[...]) + dot(l, wh[...]) + dot(h, wl[...])
        store(n).start()
        return 0

    lax.fori_loop(0, NBD * BS // STORE, chunk, 0)
    for n in range(NBD * BS // STORE):
        store(n).wait()


def orthonormalize(low, high, ah, al):
    vmem = pl.BlockSpec(memory_space=pltpu.VMEM)
    return pl.pallas_call(
        basis_kernel,
        out_shape=[
            jax.ShapeDtypeStruct((NBD * BS, K), F32),
            jax.ShapeDtypeStruct((K, K), F32),
        ],
        in_specs=[vmem] * 4,
        out_specs=[pl.BlockSpec(memory_space=pltpu.HBM), vmem],
        scratch_shapes=[
            pltpu.VMEM((K, K), BF16),
            pltpu.VMEM((K, K), BF16),
            pltpu.VMEM((NBD * BS, K), F32),
            pltpu.SemaphoreType.DMA((NBD * BS // STORE,)),
        ],
        compiler_params=pltpu.CompilerParams(vmem_limit_bytes=16 * MB),
        cost_estimate=pl.CostEstimate(flops=10**9, bytes_accessed=7 * MB, transcendentals=0),
        name="factor_and_basis",
    )(low, high, on_vmem(ah), on_vmem(al))


def body(block_vectors, stiff_tiles, col_index, send_lists, send_counts, part_blocks):
    own_blocks = block_vectors.reshape(NBD, BS, K)
    cols = col_index.reshape(NBD * TPR)
    packed = pack_ghosts(own_blocks, send_lists.reshape(4 * GMAX), send_counts.reshape(4))
    ghosts = [
        shifted(packed[0], "px", 1),
        shifted(packed[1], "px", -1),
        shifted(packed[2], "py", 1),
        shifted(packed[3], "py", -1),
    ]
    part, held, *lists = apply_own(block_vectors, stiff_tiles.reshape(NBD * TPR, BS, BS), cols, part_blocks)
    ah, al, gram = apply_ghosts(part, held, lists, ghosts)
    low, high = sum_everywhere(gram)
    return tuple(orthonormalize(low, high, ah, al))


def solution(mesh):
    placed = (
        P(AXES, None),
        P(AXES, None, None, None),
        P(AXES, None),
        P(AXES, None, None),
        P(AXES, None),
        P(AXES),
    )
    return jax.shard_map(body, mesh=mesh, in_specs=placed, out_specs=(P(AXES, None), P()), check_vma=False)
```

```python
import functools
import itertools

import jax
import jax.numpy as jnp
from jax import lax
from jax.experimental import pallas as pl
from jax.experimental.pallas import tpu as pltpu
from jax.sharding import PartitionSpec as P

AXES = ("px", "py")
SIDE = 4
BS = 128
K = 256
NBD = 24
TPR = 12
GMAX = 4
NROWS = 393216
HALF = 136
F32 = jnp.float32
BF16 = jnp.bfloat16
MB = 1 << 20
CHUNK = 8
AHEAD = 6
NEAR = 2
STORE = 512


def device_at(x, y, z, core):
    return (y * SIDE + x) * 8 + z * 2 + core


def route(move):
    places = itertools.product(range(SIDE), range(SIDE), range(SIDE), range(2))
    return [(device_at(*p), device_at(*move(*p))) for p in places]


def pair_route(dim, odd):
    def move(x, y, z, core):
        at = [x, y, z]
        v = at[dim]
        if odd:
            at[dim] = (v - 1) % SIDE if v % 2 == 0 else (v + 1) % SIDE
        else:
            at[dim] = v ^ 1
        return (*at, core)

    return route(move)


CORE_ROUTE = route(lambda x, y, z, core: (x, y, z, 1 - core))


def far_route(dim):
    def move(x, y, z, core):
        at = [x, y, z]
        at[dim] ^= 2
        return (*at, core)

    return route(move)


def swapped(block, axis, odd):
    n = lax.axis_size(axis)
    pairs = [(i, i + 1) for i in range(1 if odd else 0, n - 1, 2)]
    return lax.ppermute(block, axis, pairs + [(j, i) for i, j in pairs])


def sum_everywhere(packed):
    core = lax.axis_index("py") % 2
    mine = lax.dynamic_slice_in_dim(packed, core * HALF, HALF, 0)
    other = lax.dynamic_slice_in_dim(packed, (1 - core) * HALF, HALF, 0)
    total = mine + lax.ppermute(other, AXES, CORE_ROUTE)
    for dim in range(3):
        routes = (pair_route(dim, False), pair_route(dim, True), far_route(dim))
        near, wrap, far = [lax.ppermute(total, AXES, r) for r in routes]
        total = (total + near) + (wrap + far)
    theirs = lax.ppermute(total, AXES, CORE_ROUTE)
    low = jnp.where(core == 0, total, theirs)
    high = jnp.where(core == 0, theirs, total)
    return low, high


def on_vmem(x):
    return pltpu.with_memory_space_constraint(x, pltpu.VMEM)


def pack_kernel(parity, lists, counts, own, *refs):
    outs, held, in_sems, out_sems = refs[:4], refs[4], refs[5], refs[6]
    odd_px, odd_py = parity[0], parity[1]
    directions = (odd_px, 1 - odd_px, 2 + odd_py, 3 - odd_py)

    def fetch(n, s):
        block = lists[0, directions[n], s]
        rows = pl.ds(pl.multiple_of(block * BS, BS), BS)
        return pltpu.make_async_copy(own.at[rows], held.at[n, s], in_sems.at[n, s])

    def store(n, s):
        return pltpu.make_async_copy(held.at[n, s], outs[n].at[s], out_sems.at[n, s])

    for n in range(4):
        for s in range(GMAX):
            fetch(n, s).start()
    for n in range(4):
        for s in range(GMAX):
            fetch(n, s).wait()

            @pl.when(s >= counts[0, directions[n]])
            def _():
                held[n, s] = jnp.zeros((BS, K), F32)

            store(n, s).start()
    for n in range(4):
        for s in range(GMAX):
            store(n, s).wait()


def pack_ghosts(parity, lists, counts, own):
    smem = pl.BlockSpec(memory_space=pltpu.SMEM)
    hbm = pl.BlockSpec(memory_space=pltpu.HBM)
    anywhere = pl.BlockSpec(memory_space=pl.ANY)
    return pl.pallas_call(
        pack_kernel,
        out_shape=[jax.ShapeDtypeStruct((GMAX, BS, K), F32)] * 4,
        in_specs=[smem, smem, smem, hbm],
        out_specs=[anywhere] * 4,
        scratch_shapes=[
            pltpu.VMEM((4, GMAX, BS, K), F32),
            pltpu.SemaphoreType.DMA((4, GMAX)),
            pltpu.SemaphoreType.DMA((4, GMAX)),
        ],
        compiler_params=pltpu.CompilerParams(vmem_limit_bytes=4 * MB),
        cost_estimate=pl.CostEstimate(flops=0, bytes_accessed=4 * MB, transcendentals=0),
        name="pack_ghosts",
    )(parity, lists, counts, pltpu.with_memory_space_constraint(own, pltpu.HBM))


def split(x):
    high = x.astype(BF16)
    return high, (x - high.astype(F32)).astype(BF16)


def dot(a, b):
    return lax.dot_general(a, b, (((1,), (0,)), ((), ())), preferred_element_type=F32)


def pair_lists(parity, cols, live, own_list, ghost_list):
    turn_px, turn_py = GMAX * (1 - parity[0]), GMAX * (1 - parity[1])

    def row_pairs(row, counts):
        starts = counts
        for t in range(TPR):
            c = cols[row, t]
            ghost = jnp.where(c >= NBD, 1, 0)
            g = c - NBD
            for (tile, block, _, _), n, at in (
                (own_list, counts[0], c),
                (ghost_list, counts[1], g ^ jnp.where(g < 2 * GMAX, turn_px, turn_py)),
            ):
                tile[n] = row * TPR + t
                block[n] = at
            counts = (counts[0] + 1 - ghost, counts[1] + ghost)
        ends = []
        for (tile, block, rows, _), n, start, zero in (
            (own_list, counts[0], starts[0], NBD),
            (ghost_list, counts[1], starts[1], 4 * GMAX),
        ):
            tile[n] = 0
            block[n] = zero
            end = n + (n & 1)
            for k in range(TPR // 2):
                rows[start // 2 + k] = row
            ends.append(end)
        return tuple(ends)

    zero = jnp.int32(0)
    own_n, ghost_n = lax.fori_loop(0, live[0], row_pairs, (zero, zero))
    for (tile, block, rows, count), n, blank in (
        (own_list, own_n, NBD),
        (ghost_list, ghost_n, 4 * GMAX),
    ):
        for k in range(2 * CHUNK):
            tile[n + k] = 0
            block[n + k] = blank
        for k in range(CHUNK):
            rows[n // 2 + k] = 0
        count[0] = n // 2


def add_chunk(start, lists, tiles, xh, xl, acc):
    tile, block, rows, _ = lists
    for k in range(CHUNK):
        p = start + k
        t0, t1, c0, c1 = tile[2 * p], tile[2 * p + 1], block[2 * p], block[2 * p + 1]
        th, tl = split(jnp.concatenate([tiles[t0], tiles[t1]], axis=1))
        r0 = pl.ds(pl.multiple_of(c0 * BS, BS), BS)
        r1 = pl.ds(pl.multiple_of(c1 * BS, BS), BS)
        bh = jnp.concatenate([xh[r0], xh[r1]], axis=0)
        bl = jnp.concatenate([xl[r0], xl[r1]], axis=0)
        at = pl.ds(pl.multiple_of(rows[p] * BS, BS), BS)
        acc[at] += dot(th, bh) + dot(tl, bh) + dot(th, bl)


def own_kernel(parity, cols, live, own, tiles, part, held, gt, gb, gr, gn, xh, xl, ot, ob, orow, on, sems):
    def fetch(row):
        rows = pl.ds(row * TPR, TPR)
        return pltpu.make_async_copy(tiles.at[rows], held.at[rows], sems.at[row])

    for row in range(AHEAD):
        fetch(row).start()
    own_list, ghost_list = (ot, ob, orow, on), (gt, gb, gr, gn)
    pair_lists(parity, cols, live, own_list, ghost_list)
    part[...] = jnp.zeros_like(part)
    xh[NBD * BS :] = jnp.zeros((BS, K), BF16)
    xl[NBD * BS :] = jnp.zeros((BS, K), BF16)

    def convert(b, _):
        rows = pl.ds(pl.multiple_of(b * BS, BS), BS)
        xh[rows], xl[rows] = split(own[rows])
        return 0

    lax.fori_loop(0, NBD, convert, 0)

    def arrive(row, _):
        fetch(row).wait()

        @pl.when(row + AHEAD < NBD)
        def _():
            fetch(row + AHEAD).start()

        return 0

    pairs = on[0]

    def chunk(i, ready):
        last = jnp.minimum(i * CHUNK + CHUNK, pairs) - 1
        need = jnp.maximum(orow[last] + 1, ready)
        lax.fori_loop(ready, need, arrive, 0)
        add_chunk(i * CHUNK, own_list, held, xh, xl, part)
        return need

    ready = lax.fori_loop(0, (pairs + CHUNK - 1) // CHUNK, chunk, jnp.int32(0))
    lax.fori_loop(ready, NBD, arrive, 0)


def list_shapes(kind):
    return [
        kind((NBD * (TPR + 2) + 4 * CHUNK,), jnp.int32),
        kind((NBD * (TPR + 2) + 4 * CHUNK,), jnp.int32),
        kind((NBD * (TPR + 2) // 2 + 4 * CHUNK,), jnp.int32),
        kind((1,), jnp.int32),
    ]


def apply_own(parity, cols, live, own, tiles):
    smem = pl.BlockSpec(memory_space=pltpu.SMEM)
    vmem = pl.BlockSpec(memory_space=pltpu.VMEM)
    return pl.pallas_call(
        own_kernel,
        out_shape=[
            pltpu.VMEM((NBD * BS, K), F32),
            pltpu.VMEM((NBD * TPR, BS, BS), F32),
            *list_shapes(jax.ShapeDtypeStruct),
        ],
        in_specs=[smem, smem, smem, vmem, pl.BlockSpec(memory_space=pltpu.HBM)],
        out_specs=[vmem] * 2 + [smem] * 4,
        scratch_shapes=[
            pltpu.VMEM(((NBD + 1) * BS, K), BF16),
            pltpu.VMEM(((NBD + 1) * BS, K), BF16),
            *list_shapes(pltpu.SMEM),
            pltpu.SemaphoreType.DMA((NBD,)),
        ],
        compiler_params=pltpu.CompilerParams(vmem_limit_bytes=8 * MB),
        cost_estimate=pl.CostEstimate(flops=4 * 10**9, bytes_accessed=25 * MB, transcendentals=0),
        name="apply_own",
    )(parity, cols, live, on_vmem(own), pltpu.with_memory_space_constraint(tiles, pltpu.HBM))


def gram_pack(high, low):
    tn = lambda a, b: lax.dot_general(a, b, (((0,), (0,)), ((), ())), preferred_element_type=F32)
    main = tn(high, high)
    cross = tn(high, low)
    gram = main + cross + cross.T
    i = lax.broadcasted_iota(jnp.int32, (BS, BS), 0)
    j = lax.broadcasted_iota(jnp.int32, (BS, BS), 1)
    first, second = gram[:BS, :BS], gram[BS:, BS:]
    diagonal = jnp.sum(jnp.where(i == j, second, 0.0), axis=0, keepdims=True)
    tail = jnp.broadcast_to(diagonal, (2 * HALF - 2 * BS, BS))
    return jnp.concatenate([jnp.where(i <= j, first, second), gram[:BS, BS:], tail], axis=0)


def ghost_kernel(gt, gb, gr, gn, part, held, g0, g1, g2, g3, total, ah, al, gram, xh, xl, xv, sems):
    arrivals = [pltpu.make_async_copy(g, xv.at[e], sems.at[e]) for e, g in enumerate((g0, g1, g2, g3))]
    for c in arrivals:
        c.start()
    xh[4 * GMAX * BS :] = jnp.zeros((BS, K), BF16)
    xl[4 * GMAX * BS :] = jnp.zeros((BS, K), BF16)
    for e, c in enumerate(arrivals):
        c.wait()

        def convert(s, _):
            rows = pl.ds(pl.multiple_of((e * GMAX + s) * BS, BS), BS)
            xh[rows], xl[rows] = split(xv[e, s])
            return 0

        lax.fori_loop(0, GMAX, convert, 0)

    def chunk(i, _):
        add_chunk(i * CHUNK, (gt, gb, gr, gn), held, xh, xl, total)
        return 0

    lax.fori_loop(0, (gn[0] + CHUNK - 1) // CHUNK, chunk, 0)

    def finish(row, _):
        rows = pl.ds(pl.multiple_of(row * BS, BS), BS)
        ah[rows], al[rows] = split(total[rows])
        return 0

    lax.fori_loop(0, NBD, finish, 0)
    gram[...] = gram_pack(ah[...], al[...])


def apply_ghosts(part, held, lists, ghosts):
    smem = pl.BlockSpec(memory_space=pltpu.SMEM)
    vmem = pl.BlockSpec(memory_space=pltpu.VMEM)
    anywhere = pl.BlockSpec(memory_space=pl.ANY)
    _, ah, al, gram = pl.pallas_call(
        ghost_kernel,
        out_shape=[
            pltpu.VMEM((NBD * BS, K), F32),
            pltpu.VMEM((NBD * BS, K), BF16),
            pltpu.VMEM((NBD * BS, K), BF16),
            jax.ShapeDtypeStruct((2 * HALF, BS), F32),
        ],
        in_specs=[smem] * 4 + [vmem] * 2 + [anywhere] * 4,
        out_specs=[vmem] * 4,
        scratch_shapes=[
            pltpu.VMEM(((4 * GMAX + 1) * BS, K), BF16),
            pltpu.VMEM(((4 * GMAX + 1) * BS, K), BF16),
            pltpu.VMEM((4, GMAX, BS, K), F32),
            pltpu.SemaphoreType.DMA((4,)),
        ],
        input_output_aliases={4: 0},
        compiler_params=pltpu.CompilerParams(vmem_limit_bytes=16 * MB),
        cost_estimate=pl.CostEstimate(flops=3 * 10**9, bytes_accessed=25 * MB, transcendentals=0),
        name="apply_ghosts",
    )(*lists, on_vmem(part), on_vmem(held), *ghosts)
    return ah, al, gram


def exact(a, b, ca=1, cb=0):
    return lax.dot_general(
        a, b, (((ca,), (cb,)), ((), ())), precision=lax.Precision.HIGHEST, preferred_element_type=F32
    )


def spread(x):
    return jnp.broadcast_to(x, (8, BS))


def tree_sum(terms):
    while len(terms) > 1:
        pairs = [terms[i] + terms[i + 1] for i in range(0, len(terms) - 1, 2)]
        terms = pairs + terms[len(terms) - len(terms) % 2 :]
    return terms[0]


def eliminate(columns):
    groups, wide = BS // 8, range(len(columns))
    state = [[c[8 * g : 8 * g + 8] for c in columns] for g in range(groups)]
    outs = [[] for _ in columns]
    place = lax.broadcasted_iota(jnp.int32, (8, BS), 0)
    for at in range(groups):
        near = range(at + 1, min(groups, at + 1 + NEAR))
        first = {g: [spread(state[g][0][:, 8 * at + k : 8 * at + k + 1]) for k in range(8)] for g in (at, *near)}
        a = {(i, j): spread(first[at][j][i : i + 1]) for i in range(8) for j in range(i, 8)}
        w = [[spread(state[at][c][k : k + 1]) for c in wide] for k in range(8)]
        inverse, lower = [], {}
        for k in range(8):
            inverse.append(1.0 / a[k, k])
            for i in range(k + 1, 8):
                m = lower[i, k] = a[k, i] * inverse[k]
                for j in range(i, 8):
                    a[i, j] = a[i, j] - m * a[k, j]
                for c in wide:
                    w[i][c] = w[i][c] - m * w[k][c]
        for k in range(8):
            scale = lax.rsqrt(a[k, k])
            for c in wide:
                outs[c].append((w[k][c] * scale)[:1])
        if at + 1 == groups:
            break
        q = [[w[k][c] * inverse[k] for c in wide] for k in range(8)]
        for k in range(6, -1, -1):
            for m in range(k + 1, 8):
                for c in wide:
                    q[k][c] = q[k][c] - lower[m, k] * q[m][c]
        for g in near:
            for c in wide:
                state[g][c] = state[g][c] - tree_sum([first[g][k] * q[k][c] for k in range(8)])
        far = at + 1 + NEAR
        if far < groups:
            rows = []
            for c in wide:
                block = q[0][c]
                for k in range(1, 8):
                    block = jnp.where(place == k, q[k][c], block)
                rows.append(block)
            parts = [jnp.concatenate(rows, axis=1)]
            if at:
                parts.insert(0, jnp.zeros((8 * at, BS * len(columns)), F32))
            parts.append(jnp.zeros((BS - 8 * at - 8, BS * len(columns)), F32))
            update = exact(
                jnp.concatenate([state[g][0] for g in range(far, groups)], axis=0),
                jnp.concatenate(parts, axis=0),
            )
            for n, g in enumerate(range(far, groups)):
                for c in wide:
                    state[g][c] = state[g][c] - update[8 * n : 8 * n + 8, c * BS : c * BS + BS]
    return [jnp.concatenate(rows, axis=0) for rows in outs]


def factor(low, high):
    packed = jnp.concatenate([low, high], axis=0) * (1.0 / NROWS)
    mixed, corner, tail = packed[:BS], packed[BS : 2 * BS], packed[2 * BS : 2 * BS + 1]
    i = lax.broadcasted_iota(jnp.int32, (BS, BS), 0)
    j = lax.broadcasted_iota(jnp.int32, (BS, BS), 1)
    unit = jnp.where(i == j, 1.0, 0.0).astype(F32)
    turned = mixed.T
    first = jnp.where(i <= j, mixed, turned)
    second = jnp.where(i > j, mixed, jnp.where(i < j, turned, tail))
    r11, r12, x11 = eliminate([first, corner, unit])
    x11 = jnp.where(i >= j, x11, 0.0)
    r22, x22 = eliminate([second - exact(r12, r12, 0, 0), unit])
    x22 = jnp.where(i >= j, x22, 0.0)
    x21 = -exact(x22, exact(r12, x11, 0, 0))
    r11, r22 = jnp.where(i <= j, r11, 0.0), jnp.where(i <= j, r22, 0.0)
    zero = jnp.zeros((BS, BS), F32)
    upper = jnp.concatenate(
        [jnp.concatenate([r11, r12], axis=1), jnp.concatenate([zero, r22], axis=1)], axis=0
    )
    lower = jnp.concatenate(
        [jnp.concatenate([x11, zero], axis=1), jnp.concatenate([x21, x22], axis=1)], axis=0
    )
    return upper, lower


def basis_kernel(low, high, ah, al, basis, upper, wh, wl, staged, sems):
    r, x = factor(low[...], high[...])
    upper[...] = r
    wh[...], wl[...] = split(x.T)

    def store(n):
        rows = pl.ds(pl.multiple_of(n * STORE, STORE), STORE)
        return pltpu.make_async_copy(staged.at[rows], basis.at[rows], sems.at[n])

    def chunk(n, _):
        rows = pl.ds(pl.multiple_of(n * STORE, STORE), STORE)
        h, l = ah[rows], al[rows]
        staged[rows] = dot(h, wh[...]) + dot(l, wh[...]) + dot(h, wl[...])
        store(n).start()
        return 0

    lax.fori_loop(0, NBD * BS // STORE, chunk, 0)
    for n in range(NBD * BS // STORE):
        store(n).wait()


def orthonormalize(low, high, ah, al):
    vmem = pl.BlockSpec(memory_space=pltpu.VMEM)
    return pl.pallas_call(
        basis_kernel,
        out_shape=[
            jax.ShapeDtypeStruct((NBD * BS, K), F32),
            jax.ShapeDtypeStruct((K, K), F32),
        ],
        in_specs=[vmem] * 4,
        out_specs=[pl.BlockSpec(memory_space=pltpu.HBM), vmem],
        scratch_shapes=[
            pltpu.VMEM((K, K), BF16),
            pltpu.VMEM((K, K), BF16),
            pltpu.VMEM((NBD * BS, K), F32),
            pltpu.SemaphoreType.DMA((NBD * BS // STORE,)),
        ],
        compiler_params=pltpu.CompilerParams(vmem_limit_bytes=16 * MB),
        cost_estimate=pl.CostEstimate(flops=10**9, bytes_accessed=7 * MB, transcendentals=0),
        name="factor_and_basis",
    )(low, high, on_vmem(ah), on_vmem(al))


def body(block_vectors, stiff_tiles, col_index, send_lists, send_counts, part_blocks):
    parity = jnp.stack([lax.axis_index("px") % 2, lax.axis_index("py") % 2]).astype(jnp.int32)
    tiles = stiff_tiles.reshape(NBD * TPR, BS, BS)
    packed = pack_ghosts(parity, send_lists, send_counts, block_vectors)
    ghosts = [
        swapped(packed[0], "px", False),
        swapped(packed[1], "px", True),
        swapped(packed[2], "py", False),
        swapped(packed[3], "py", True),
    ]
    part, held, *lists = apply_own(parity, col_index, part_blocks, block_vectors, tiles)
    ah, al, gram = apply_ghosts(part, held, lists, ghosts)
    low, high = sum_everywhere(gram)
    return tuple(orthonormalize(low, high, ah, al))


def solution(mesh):
    placed = (
        P(AXES, None),
        P(AXES, None, None, None),
        P(AXES, None),
        P(AXES, None, None),
        P(AXES, None),
        P(AXES),
    )
    return jax.shard_map(body, mesh=mesh, in_specs=placed, out_specs=(P(AXES, None), P()), check_vma=False)
```

```python
import functools
import itertools

import jax
import jax.numpy as jnp
from jax import lax
from jax.experimental import pallas as pl
from jax.experimental.pallas import tpu as pltpu
from jax.sharding import PartitionSpec as P

AXES = ("px", "py")
SIDE = 4
BS = 128
K = 256
NBD = 24
TPR = 12
GMAX = 4
NROWS = 393216
HALF = 136
F32 = jnp.float32
BF16 = jnp.bfloat16
MB = 1 << 20
OWN_CHUNK = 8
GHOST_CHUNK = 12
LIST_AT = 8
LIST_SIZE = LIST_AT + NBD * TPR + 2 * NBD + 32
TILE_SHIFT = 6
ROW_SHIFT = 16
TILE_UNIT = 1 << TILE_SHIFT
ROW_UNIT = 1 << ROW_SHIFT
AHEAD = 9
NEAR = 2
STORE = 1024


def device_at(x, y, z, core):
    return (y * SIDE + x) * 8 + z * 2 + core


def route(move):
    places = itertools.product(range(SIDE), range(SIDE), range(SIDE), range(2))
    return [(device_at(*p), device_at(*move(*p))) for p in places]


def pair_route(dim, odd):
    def move(x, y, z, core):
        at = [x, y, z]
        v = at[dim]
        if odd:
            at[dim] = (v - 1) % SIDE if v % 2 == 0 else (v + 1) % SIDE
        else:
            at[dim] = v ^ 1
        return (*at, core)

    return route(move)


CORE_ROUTE = route(lambda x, y, z, core: (x, y, z, 1 - core))


def far_route(dim):
    def move(x, y, z, core):
        at = [x, y, z]
        at[dim] ^= 2
        return (*at, core)

    return route(move)


def swapped(block, axis, odd):
    n = lax.axis_size(axis)
    pairs = [(i, i + 1) for i in range(1 if odd else 0, n - 1, 2)]
    return lax.ppermute(block, axis, pairs + [(j, i) for i, j in pairs])


def sum_everywhere(packed):
    core = lax.axis_index("py") % 2
    mine = lax.dynamic_slice_in_dim(packed, core * HALF, HALF, 0)
    other = lax.dynamic_slice_in_dim(packed, (1 - core) * HALF, HALF, 0)
    total = mine + lax.ppermute(other, AXES, CORE_ROUTE)
    for dim in range(3):
        routes = (pair_route(dim, False), pair_route(dim, True), far_route(dim))
        near, wrap, far = [lax.ppermute(total, AXES, r) for r in routes]
        total = (total + near) + (wrap + far)
    theirs = lax.ppermute(total, AXES, CORE_ROUTE)
    low = jnp.where(core == 0, total, theirs)
    high = jnp.where(core == 0, theirs, total)
    return low, high


def on_vmem(x):
    return pltpu.with_memory_space_constraint(x, pltpu.VMEM)


def split(x):
    high = x.astype(BF16)
    return high, (x - high.astype(F32)).astype(BF16)


def dot(a, b):
    return lax.dot_general(a, b, (((1,), (0,)), ((), ())), preferred_element_type=F32)


def pair_lists(parity, cols, live, own_list, ghost_list):
    turn_px, turn_py = GMAX * (1 - parity[0]), GMAX * (1 - parity[1])

    def row_pairs(row, counts):
        own_n, ghost_n = counts
        base = row * (ROW_UNIT + TPR * TILE_UNIT)
        for t in range(TPR):
            c = cols[t, row]
            ghost = jnp.where(c >= NBD, 1, 0)
            g = c - NBD
            entry = base + t * TILE_UNIT
            own_list[LIST_AT + own_n] = entry + c
            ghost_list[LIST_AT + ghost_n] = entry + (g ^ jnp.where(g < 2 * GMAX, turn_px, turn_py))
            own_n, ghost_n = own_n + 1 - ghost, ghost_n + ghost
        own_list[LIST_AT + own_n] = NBD
        ghost_list[LIST_AT + ghost_n] = 4 * GMAX
        return own_n + (own_n & 1), ghost_n + (ghost_n & 1)

    zero = jnp.int32(0)
    ends = lax.fori_loop(0, live[0], row_pairs, (zero, zero))
    for out, n, blank, chunk in (
        (own_list, ends[0], NBD, OWN_CHUNK),
        (ghost_list, ends[1], 4 * GMAX, GHOST_CHUNK),
    ):
        for k in range(2 * chunk):
            out[LIST_AT + n + k] = blank
        out[0] = n >> 1


def prepare_kernel(parity, live, lists_in, counts_in, cols_in, own, *refs):
    outs, (own_list, ghost_list, lists, counts, cols, held) = refs[:4], refs[4:10]
    small_sems, in_sems, out_sems = refs[10:]
    small = [
        pltpu.make_async_copy(a, b, small_sems.at[n])
        for n, (a, b) in enumerate(((lists_in, lists), (counts_in, counts), (cols_in, cols)))
    ]
    for c in small:
        c.start()
    odd_px, odd_py = parity[0], parity[1]
    directions = (1 - odd_px, odd_px, 3 - odd_py, 2 + odd_py)

    def fetch(n, s):
        block = lists[0, directions[n], s]
        rows = pl.ds(pl.multiple_of(block * BS, BS), BS)
        return pltpu.make_async_copy(own.at[rows], held.at[n, s], in_sems.at[n, s])

    def store(n, s):
        return pltpu.make_async_copy(held.at[n, s], outs[n].at[s], out_sems.at[n, s])

    small[0].wait()
    for n in range(4):
        for s in range(GMAX):
            fetch(n, s).start()
    for c in small[1:]:
        c.wait()
    pair_lists(parity, cols, live, own_list, ghost_list)
    for n in range(4):
        for s in range(GMAX):
            fetch(n, s).wait()

            @pl.when(s >= counts[0, directions[n]])
            def _():
                held[n, s] = jnp.zeros((BS, K), F32)

            store(n, s).start()
    for n in range(4):
        for s in range(GMAX):
            store(n, s).wait()


def prepare(parity, lists, counts, cols, live, own):
    smem = pl.BlockSpec(memory_space=pltpu.SMEM)
    hbm = pl.BlockSpec(memory_space=pltpu.HBM)
    anywhere = pl.BlockSpec(memory_space=pl.ANY)
    arrays = (lists, counts, cols, own)
    outs = pl.pallas_call(
        prepare_kernel,
        out_shape=[jax.ShapeDtypeStruct((GMAX, BS, K), F32)] * 4
        + [jax.ShapeDtypeStruct((LIST_SIZE,), jnp.int32)] * 2,
        in_specs=[smem] * 2 + [hbm] * 4,
        out_specs=[anywhere] * 4 + [smem] * 2,
        scratch_shapes=[
            *[pltpu.SMEM(a.shape, jnp.int32) for a in arrays[:3]],
            pltpu.VMEM((4, GMAX, BS, K), F32),
            pltpu.SemaphoreType.DMA((3,)),
            pltpu.SemaphoreType.DMA((4, GMAX)),
            pltpu.SemaphoreType.DMA((4, GMAX)),
        ],
        compiler_params=pltpu.CompilerParams(vmem_limit_bytes=4 * MB),
        cost_estimate=pl.CostEstimate(flops=0, bytes_accessed=4 * MB, transcendentals=0),
        name="prepare",
    )(parity, live, *[pltpu.with_memory_space_constraint(a, pltpu.HBM) for a in arrays])
    return outs[:4], outs[4:]


def add_chunk(start, size, pairs, tiles, xh, xl, acc):
    for k in range(size):
        first = pairs[LIST_AT + 2 * (start + k)]
        second = pairs[LIST_AT + 2 * (start + k) + 1]
        t0, t1 = (first >> TILE_SHIFT) & 1023, (second >> TILE_SHIFT) & 1023
        c0, c1 = first & 63, second & 63
        th, tl = split(jnp.concatenate([tiles[t0], tiles[t1]], axis=1))
        r0 = pl.ds(pl.multiple_of(c0 * BS, BS), BS)
        r1 = pl.ds(pl.multiple_of(c1 * BS, BS), BS)
        bh = jnp.concatenate([xh[r0], xh[r1]], axis=0)
        bl = jnp.concatenate([xl[r0], xl[r1]], axis=0)
        at = pl.ds(pl.multiple_of((first >> ROW_SHIFT) * BS, BS), BS)
        acc[at] += dot(th, bh) + dot(tl, bh) + dot(th, bl)


def own_kernel(pairs, own, tiles, part, held, xh, xl, sems):
    def fetch(row):
        rows = pl.ds(row * TPR, TPR)
        return pltpu.make_async_copy(tiles.at[rows], held.at[rows], sems.at[row])

    for row in range(AHEAD):
        fetch(row).start()
    xh[NBD * BS :] = jnp.zeros((BS, K), BF16)
    xl[NBD * BS :] = jnp.zeros((BS, K), BF16)

    def convert(b, _):
        rows = pl.ds(pl.multiple_of(b * BS, BS), BS)
        xh[rows], xl[rows] = split(own[rows])
        part[rows] = jnp.zeros((BS, K), F32)
        return 0

    lax.fori_loop(0, NBD, convert, 0)

    def arrive(row, _):
        fetch(row).wait()

        @pl.when(row + AHEAD < NBD)
        def _():
            fetch(row + AHEAD).start()

        return 0

    count = pairs[0]

    def chunk(i, ready):
        last = jnp.minimum(i * OWN_CHUNK + OWN_CHUNK, count) - 1
        need = jnp.maximum((pairs[LIST_AT + 2 * last] >> ROW_SHIFT) + 1, ready)
        lax.fori_loop(ready, need, arrive, 0)
        add_chunk(i * OWN_CHUNK, OWN_CHUNK, pairs, held, xh, xl, part)
        return need

    ready = lax.fori_loop(0, (count + OWN_CHUNK - 1) // OWN_CHUNK, chunk, jnp.int32(0))
    lax.fori_loop(ready, NBD, arrive, 0)


def apply_own(pairs, own, tiles):
    vmem = pl.BlockSpec(memory_space=pltpu.VMEM)
    return pl.pallas_call(
        own_kernel,
        out_shape=[pltpu.VMEM((NBD * BS, K), F32), pltpu.VMEM((NBD * TPR, BS, BS), F32)],
        in_specs=[pl.BlockSpec(memory_space=pltpu.SMEM), vmem, pl.BlockSpec(memory_space=pltpu.HBM)],
        out_specs=[vmem] * 2,
        scratch_shapes=[
            pltpu.VMEM(((NBD + 1) * BS, K), BF16),
            pltpu.VMEM(((NBD + 1) * BS, K), BF16),
            pltpu.SemaphoreType.DMA((NBD,)),
        ],
        compiler_params=pltpu.CompilerParams(vmem_limit_bytes=8 * MB),
        cost_estimate=pl.CostEstimate(flops=4 * 10**9, bytes_accessed=25 * MB, transcendentals=0),
        name="apply_own",
    )(pairs, on_vmem(own), pltpu.with_memory_space_constraint(tiles, pltpu.HBM))


def gram_pack(high, low):
    tn = lambda a, b: lax.dot_general(a, b, (((0,), (0,)), ((), ())), preferred_element_type=F32)
    main = tn(high, high)
    cross = tn(high, low)
    gram = main + cross + cross.T
    i = lax.broadcasted_iota(jnp.int32, (BS, BS), 0)
    j = lax.broadcasted_iota(jnp.int32, (BS, BS), 1)
    first, second = gram[:BS, :BS], gram[BS:, BS:]
    diagonal = jnp.sum(jnp.where(i == j, second, 0.0), axis=0, keepdims=True)
    tail = jnp.broadcast_to(diagonal, (2 * HALF - 2 * BS, BS))
    return jnp.concatenate([jnp.where(i <= j, first, second), gram[:BS, BS:], tail], axis=0)


def ghost_kernel(pairs, _, held, g0, g1, g2, g3, total, high, low, gram, xh, xl, xv, ah, al, sems, out_sems):
    arrivals = [pltpu.make_async_copy(g, xv.at[e], sems.at[e]) for e, g in enumerate((g0, g1, g2, g3))]
    for c in arrivals:
        c.start()
    xh[4 * GMAX * BS :] = jnp.zeros((BS, K), BF16)
    xl[4 * GMAX * BS :] = jnp.zeros((BS, K), BF16)
    for e, c in enumerate(arrivals):
        c.wait()

        def convert(s, _):
            rows = pl.ds(pl.multiple_of((e * GMAX + s) * BS, BS), BS)
            xh[rows], xl[rows] = split(xv[e, s])
            return 0

        lax.fori_loop(0, GMAX, convert, 0)

    def chunk(i, _):
        add_chunk(i * GHOST_CHUNK, GHOST_CHUNK, pairs, held, xh, xl, total)
        return 0

    lax.fori_loop(0, (pairs[0] + GHOST_CHUNK - 1) // GHOST_CHUNK, chunk, 0)

    def finish(row, _):
        rows = pl.ds(pl.multiple_of(row * BS, BS), BS)
        ah[rows], al[rows] = split(total[rows])
        return 0

    lax.fori_loop(0, NBD, finish, 0)
    stores = [pltpu.make_async_copy(a, b, out_sems.at[n]) for n, (a, b) in enumerate(((ah, high), (al, low)))]
    for c in stores:
        c.start()
    gram[...] = gram_pack(ah[...], al[...])
    for c in stores:
        c.wait()


def apply_ghosts(pairs, part, held, ghosts):
    smem = pl.BlockSpec(memory_space=pltpu.SMEM)
    vmem = pl.BlockSpec(memory_space=pltpu.VMEM)
    anywhere = pl.BlockSpec(memory_space=pl.ANY)
    hbm = pl.BlockSpec(memory_space=pltpu.HBM)
    _, ah, al, gram = pl.pallas_call(
        ghost_kernel,
        out_shape=[
            pltpu.VMEM((NBD * BS, K), F32),
            pltpu.HBM((NBD * BS, K), BF16),
            pltpu.HBM((NBD * BS, K), BF16),
            jax.ShapeDtypeStruct((2 * HALF, BS), F32),
        ],
        in_specs=[smem] + [vmem] * 2 + [anywhere] * 4,
        out_specs=[vmem, hbm, hbm, vmem],
        scratch_shapes=[
            pltpu.VMEM(((4 * GMAX + 1) * BS, K), BF16),
            pltpu.VMEM(((4 * GMAX + 1) * BS, K), BF16),
            pltpu.VMEM((4, GMAX, BS, K), F32),
            pltpu.VMEM((NBD * BS, K), BF16),
            pltpu.VMEM((NBD * BS, K), BF16),
            pltpu.SemaphoreType.DMA((4,)),
            pltpu.SemaphoreType.DMA((2,)),
        ],
        input_output_aliases={1: 0},
        compiler_params=pltpu.CompilerParams(vmem_limit_bytes=12 * MB),
        cost_estimate=pl.CostEstimate(flops=3 * 10**9, bytes_accessed=25 * MB, transcendentals=0),
        name="apply_ghosts",
    )(pairs, on_vmem(part), on_vmem(held), *ghosts)
    return ah, al, gram


def exact(a, b, ca=1, cb=0):
    return lax.dot_general(
        a, b, (((ca,), (cb,)), ((), ())), precision=lax.Precision.HIGHEST, preferred_element_type=F32
    )


def spread(x):
    return jnp.broadcast_to(x, (8, BS))


def tree_sum(terms):
    while len(terms) > 1:
        pairs = [terms[i] + terms[i + 1] for i in range(0, len(terms) - 1, 2)]
        terms = pairs + terms[len(terms) - len(terms) % 2 :]
    return terms[0]


def eliminate(columns):
    groups, wide = BS // 8, range(len(columns))
    state = [[c[8 * g : 8 * g + 8] for c in columns] for g in range(groups)]
    outs = [[] for _ in columns]
    place = lax.broadcasted_iota(jnp.int32, (8, BS), 0)
    for at in range(groups):
        near = range(at + 1, min(groups, at + 1 + NEAR))
        first = {g: [spread(state[g][0][:, 8 * at + k : 8 * at + k + 1]) for k in range(8)] for g in (at, *near)}
        a = {(i, j): spread(first[at][j][i : i + 1]) for i in range(8) for j in range(i, 8)}
        w = [[spread(state[at][c][k : k + 1]) for c in wide] for k in range(8)]
        inverse, lower = [], {}
        for k in range(8):
            inverse.append(1.0 / a[k, k])
            for i in range(k + 1, 8):
                m = lower[i, k] = a[k, i] * inverse[k]
                for j in range(i, 8):
                    a[i, j] = a[i, j] - m * a[k, j]
                for c in wide:
                    w[i][c] = w[i][c] - m * w[k][c]
        for k in range(8):
            scale = lax.rsqrt(a[k, k])
            for c in wide:
                outs[c].append((w[k][c] * scale)[:1])
        if at + 1 == groups:
            break
        q = [[w[k][c] * inverse[k] for c in wide] for k in range(8)]
        for k in range(6, -1, -1):
            for m in range(k + 1, 8):
                for c in wide:
                    q[k][c] = q[k][c] - lower[m, k] * q[m][c]
        for g in near:
            for c in wide:
                state[g][c] = state[g][c] - tree_sum([first[g][k] * q[k][c] for k in range(8)])
        far = at + 1 + NEAR
        if far < groups:
            rows = []
            for c in wide:
                block = q[0][c]
                for k in range(1, 8):
                    block = jnp.where(place == k, q[k][c], block)
                rows.append(block)
            parts = [jnp.concatenate(rows, axis=1)]
            if at:
                parts.insert(0, jnp.zeros((8 * at, BS * len(columns)), F32))
            parts.append(jnp.zeros((BS - 8 * at - 8, BS * len(columns)), F32))
            update = exact(
                jnp.concatenate([state[g][0] for g in range(far, groups)], axis=0),
                jnp.concatenate(parts, axis=0),
            )
            for n, g in enumerate(range(far, groups)):
                for c in wide:
                    state[g][c] = state[g][c] - update[8 * n : 8 * n + 8, c * BS : c * BS + BS]
    return [jnp.concatenate(rows, axis=0) for rows in outs]


def factor(low, high):
    packed = jnp.concatenate([low, high], axis=0) * (1.0 / NROWS)
    mixed, corner, tail = packed[:BS], packed[BS : 2 * BS], packed[2 * BS : 2 * BS + 1]
    i = lax.broadcasted_iota(jnp.int32, (BS, BS), 0)
    j = lax.broadcasted_iota(jnp.int32, (BS, BS), 1)
    unit = jnp.where(i == j, 1.0, 0.0).astype(F32)
    turned = mixed.T
    first = jnp.where(i <= j, mixed, turned)
    second = jnp.where(i > j, mixed, jnp.where(i < j, turned, tail))
    r11, r12, x11 = eliminate([first, corner, unit])
    x11 = jnp.where(i >= j, x11, 0.0)
    r22, x22 = eliminate([second - exact(r12, r12, 0, 0), unit])
    x22 = jnp.where(i >= j, x22, 0.0)
    x21 = -exact(x22, exact(r12, x11, 0, 0))
    r11, r22 = jnp.where(i <= j, r11, 0.0), jnp.where(i <= j, r22, 0.0)
    zero = jnp.zeros((BS, BS), F32)
    upper = jnp.concatenate(
        [jnp.concatenate([r11, r12], axis=1), jnp.concatenate([zero, r22], axis=1)], axis=0
    )
    lower = jnp.concatenate(
        [jnp.concatenate([x11, zero], axis=1), jnp.concatenate([x21, x22], axis=1)], axis=0
    )
    return upper, lower


def basis_kernel(low, high, rows_high, rows_low, basis, upper, wh, wl, ah, al, staged, in_sems, sems):
    pieces = NBD * BS // STORE

    def piece(n):
        return pl.ds(pl.multiple_of(n * STORE, STORE), STORE)

    def load(n):
        rows = piece(n)
        return [
            pltpu.make_async_copy(a.at[rows], b.at[rows], in_sems.at[k, n])
            for k, (a, b) in enumerate(((rows_high, ah), (rows_low, al)))
        ]

    def store(n):
        return pltpu.make_async_copy(staged.at[piece(n)], basis.at[piece(n)], sems.at[n])

    def begin(n, _):
        for c in load(n):
            c.start()
        return 0

    lax.fori_loop(0, pieces, begin, 0)
    r, x = factor(low[...], high[...])
    upper[...] = r
    wh[...], wl[...] = split(x.T)

    def multiply(n, _):
        for c in load(n):
            c.wait()
        rows = piece(n)
        h, l = ah[rows], al[rows]
        staged[rows] = dot(h, wh[...]) + dot(l, wh[...]) + dot(h, wl[...])
        store(n).start()
        return 0

    lax.fori_loop(0, pieces, multiply, 0)
    for n in range(pieces):
        store(n).wait()


def orthonormalize(low, high, ah, al):
    vmem = pl.BlockSpec(memory_space=pltpu.VMEM)
    hbm = pl.BlockSpec(memory_space=pltpu.HBM)
    return pl.pallas_call(
        basis_kernel,
        out_shape=[
            jax.ShapeDtypeStruct((NBD * BS, K), F32),
            jax.ShapeDtypeStruct((K, K), F32),
        ],
        in_specs=[vmem] * 2 + [hbm] * 2,
        out_specs=[hbm, vmem],
        scratch_shapes=[
            pltpu.VMEM((K, K), BF16),
            pltpu.VMEM((K, K), BF16),
            pltpu.VMEM((NBD * BS, K), BF16),
            pltpu.VMEM((NBD * BS, K), BF16),
            pltpu.VMEM((NBD * BS, K), F32),
            pltpu.SemaphoreType.DMA((2, NBD * BS // STORE)),
            pltpu.SemaphoreType.DMA((NBD * BS // STORE,)),
        ],
        compiler_params=pltpu.CompilerParams(vmem_limit_bytes=12 * MB),
        cost_estimate=pl.CostEstimate(flops=10**9, bytes_accessed=7 * MB, transcendentals=0),
        name="factor_and_basis",
    )(low, high, *[pltpu.with_memory_space_constraint(a, pltpu.HBM) for a in (ah, al)])


def body(block_vectors, stiff_tiles, col_index, send_lists, send_counts, part_blocks):
    parity = jnp.stack([lax.axis_index("px") % 2, lax.axis_index("py") % 2]).astype(jnp.int32)
    tiles = stiff_tiles.reshape(NBD * TPR, BS, BS)
    (px_odd, px_even, py_odd, py_even), (own_pairs, ghost_pairs) = prepare(
        parity, send_lists, send_counts, col_index.T, part_blocks, block_vectors
    )
    px_odd = swapped(px_odd, "px", True)
    py_even = swapped(py_even, "py", False)
    px_even = swapped(px_even, "px", False)
    py_odd = swapped(py_odd, "py", True)
    part, held = apply_own(own_pairs, block_vectors, tiles)
    ah, al, gram = apply_ghosts(ghost_pairs, part, held, [px_even, px_odd, py_even, py_odd])
    low, high = sum_everywhere(gram)
    return tuple(orthonormalize(low, high, ah, al))


def solution(mesh):
    placed = (
        P(AXES, None),
        P(AXES, None, None, None),
        P(AXES, None),
        P(AXES, None, None),
        P(AXES, None),
        P(AXES),
    )
    return jax.shard_map(body, mesh=mesh, in_specs=placed, out_specs=(P(AXES, None), P()), check_vma=False)
```

```python
import functools
import itertools

import jax
import jax.numpy as jnp
from jax import lax
from jax.experimental import pallas as pl
from jax.experimental.pallas import tpu as pltpu
from jax.sharding import PartitionSpec as P

AXES = ("px", "py")
SIDE = 4
BS = 128
K = 256
NBD = 24
TPR = 12
GMAX = 4
NROWS = 393216
HALF = 136
F32 = jnp.float32
BF16 = jnp.bfloat16
MB = 1 << 20
OWN_CHUNK = 8
GHOST_CHUNK = 12
LIST_AT = 8
LIST_SIZE = LIST_AT + NBD * TPR + 2 * NBD + 32
TILE_SHIFT = 6
ROW_SHIFT = 16
TILE_UNIT = 1 << TILE_SHIFT
ROW_UNIT = 1 << ROW_SHIFT
AHEAD = 9
NEAR = 2
STORE = 1024


def device_at(x, y, z, core):
    return (y * SIDE + x) * 8 + z * 2 + core


def route(move):
    places = itertools.product(range(SIDE), range(SIDE), range(SIDE), range(2))
    return [(device_at(*p), device_at(*move(*p))) for p in places]


def pair_route(dim, odd):
    def move(x, y, z, core):
        at = [x, y, z]
        v = at[dim]
        if odd:
            at[dim] = (v - 1) % SIDE if v % 2 == 0 else (v + 1) % SIDE
        else:
            at[dim] = v ^ 1
        return (*at, core)

    return route(move)


CORE_ROUTE = route(lambda x, y, z, core: (x, y, z, 1 - core))


def far_route(dim):
    def move(x, y, z, core):
        at = [x, y, z]
        at[dim] ^= 2
        return (*at, core)

    return route(move)


def swapped(block, axis, odd):
    n = lax.axis_size(axis)
    pairs = [(i, i + 1) for i in range(1 if odd else 0, n - 1, 2)]
    return lax.ppermute(block, axis, pairs + [(j, i) for i, j in pairs])


def sum_everywhere(packed):
    core = lax.axis_index("py") % 2
    mine = lax.dynamic_slice_in_dim(packed, core * HALF, HALF, 0)
    other = lax.dynamic_slice_in_dim(packed, (1 - core) * HALF, HALF, 0)
    total = mine + lax.ppermute(other, AXES, CORE_ROUTE)
    for dim in range(3):
        routes = [pair_route(dim, False), pair_route(dim, True), far_route(dim)]
        if dim == 1:
            routes = routes[1:] + routes[:1]
        first, second, third = [lax.ppermute(total, AXES, r) for r in routes]
        total = (total + first) + (second + third)
    theirs = lax.ppermute(total, AXES, CORE_ROUTE)
    low = jnp.where(core == 0, total, theirs)
    high = jnp.where(core == 0, theirs, total)
    return low, high


def on_vmem(x):
    return pltpu.with_memory_space_constraint(x, pltpu.VMEM)


def split(x):
    high = x.astype(BF16)
    return high, (x - high.astype(F32)).astype(BF16)


def dot(a, b):
    return lax.dot_general(a, b, (((1,), (0,)), ((), ())), preferred_element_type=F32)


def pair_lists(parity, cols, live, own_list, ghost_list):
    turn_px, turn_py = GMAX * (1 - parity[0]), GMAX * (1 - parity[1])

    def row_pairs(row, counts):
        own_n, ghost_n = counts
        base = row * (ROW_UNIT + TPR * TILE_UNIT)
        for t in range(TPR):
            c = cols[t, row]
            ghost = jnp.where(c >= NBD, 1, 0)
            g = c - NBD
            entry = base + t * TILE_UNIT
            own_list[LIST_AT + own_n] = entry + c
            ghost_list[LIST_AT + ghost_n] = entry + (g ^ jnp.where(g < 2 * GMAX, turn_px, turn_py))
            own_n, ghost_n = own_n + 1 - ghost, ghost_n + ghost
        own_list[LIST_AT + own_n] = NBD
        ghost_list[LIST_AT + ghost_n] = 4 * GMAX
        return own_n + (own_n & 1), ghost_n + (ghost_n & 1)

    zero = jnp.int32(0)
    ends = lax.fori_loop(0, live[0], row_pairs, (zero, zero))
    for out, n, blank, chunk in (
        (own_list, ends[0], NBD, OWN_CHUNK),
        (ghost_list, ends[1], 4 * GMAX, GHOST_CHUNK),
    ):
        for k in range(2 * chunk):
            out[LIST_AT + n + k] = blank
        out[0] = n >> 1


def prepare_kernel(parity, live, lists_in, counts_in, cols_in, own, *refs):
    outs, (own_list, ghost_list, lists, counts, cols, held) = refs[:4], refs[4:10]
    small_sems, in_sems, out_sems = refs[10:]
    small = [
        pltpu.make_async_copy(a, b, small_sems.at[n])
        for n, (a, b) in enumerate(((lists_in, lists), (counts_in, counts), (cols_in, cols)))
    ]
    for c in small:
        c.start()
    odd_px, odd_py = parity[0], parity[1]
    directions = (1 - odd_px, odd_px, 3 - odd_py, 2 + odd_py)

    def fetch(n, s):
        block = lists[0, directions[n], s]
        rows = pl.ds(pl.multiple_of(block * BS, BS), BS)
        return pltpu.make_async_copy(own.at[rows], held.at[n, s], in_sems.at[n, s])

    def store(n, s):
        return pltpu.make_async_copy(held.at[n, s], outs[n].at[s], out_sems.at[n, s])

    small[0].wait()
    for n in range(4):
        for s in range(GMAX):
            fetch(n, s).start()
    for c in small[1:]:
        c.wait()
    pair_lists(parity, cols, live, own_list, ghost_list)
    for n in range(4):
        for s in range(GMAX):
            fetch(n, s).wait()

            @pl.when(s >= counts[0, directions[n]])
            def _():
                held[n, s] = jnp.zeros((BS, K), F32)

            store(n, s).start()
    for n in range(4):
        for s in range(GMAX):
            store(n, s).wait()


def prepare(parity, lists, counts, cols, live, own):
    smem = pl.BlockSpec(memory_space=pltpu.SMEM)
    hbm = pl.BlockSpec(memory_space=pltpu.HBM)
    anywhere = pl.BlockSpec(memory_space=pl.ANY)
    arrays = (lists, counts, cols, own)
    outs = pl.pallas_call(
        prepare_kernel,
        out_shape=[jax.ShapeDtypeStruct((GMAX, BS, K), F32)] * 4
        + [jax.ShapeDtypeStruct((LIST_SIZE,), jnp.int32)] * 2,
        in_specs=[smem] * 2 + [hbm] * 4,
        out_specs=[anywhere] * 4 + [smem] * 2,
        scratch_shapes=[
            *[pltpu.SMEM(a.shape, jnp.int32) for a in arrays[:3]],
            pltpu.VMEM((4, GMAX, BS, K), F32),
            pltpu.SemaphoreType.DMA((3,)),
            pltpu.SemaphoreType.DMA((4, GMAX)),
            pltpu.SemaphoreType.DMA((4, GMAX)),
        ],
        compiler_params=pltpu.CompilerParams(vmem_limit_bytes=4 * MB),
        cost_estimate=pl.CostEstimate(flops=0, bytes_accessed=4 * MB, transcendentals=0),
        name="prepare",
    )(parity, live, *[pltpu.with_memory_space_constraint(a, pltpu.HBM) for a in arrays])
    return outs[:4], outs[4:]


def add_chunk(start, size, pairs, tiles, xh, xl, acc):
    for k in range(size):
        first = pairs[LIST_AT + 2 * (start + k)]
        second = pairs[LIST_AT + 2 * (start + k) + 1]
        t0, t1 = (first >> TILE_SHIFT) & 1023, (second >> TILE_SHIFT) & 1023
        c0, c1 = first & 63, second & 63
        th, tl = split(jnp.concatenate([tiles[t0], tiles[t1]], axis=1))
        r0 = pl.ds(pl.multiple_of(c0 * BS, BS), BS)
        r1 = pl.ds(pl.multiple_of(c1 * BS, BS), BS)
        bh = jnp.concatenate([xh[r0], xh[r1]], axis=0)
        bl = jnp.concatenate([xl[r0], xl[r1]], axis=0)
        at = pl.ds(pl.multiple_of((first >> ROW_SHIFT) * BS, BS), BS)
        acc[at] += dot(th, bh) + dot(tl, bh) + dot(th, bl)


def own_kernel(pairs, own, tiles, part, held, xh, xl, sems):
    def fetch(row):
        rows = pl.ds(row * TPR, TPR)
        return pltpu.make_async_copy(tiles.at[rows], held.at[rows], sems.at[row])

    for row in range(AHEAD):
        fetch(row).start()
    xh[NBD * BS :] = jnp.zeros((BS, K), BF16)
    xl[NBD * BS :] = jnp.zeros((BS, K), BF16)

    def convert(b, _):
        rows = pl.ds(pl.multiple_of(b * BS, BS), BS)
        xh[rows], xl[rows] = split(own[rows])
        part[rows] = jnp.zeros((BS, K), F32)
        return 0

    lax.fori_loop(0, NBD, convert, 0)

    def arrive(row, _):
        fetch(row).wait()

        @pl.when(row + AHEAD < NBD)
        def _():
            fetch(row + AHEAD).start()

        return 0

    count = pairs[0]

    def chunk(i, ready):
        last = jnp.minimum(i * OWN_CHUNK + OWN_CHUNK, count) - 1
        need = jnp.maximum((pairs[LIST_AT + 2 * last] >> ROW_SHIFT) + 1, ready)
        lax.fori_loop(ready, need, arrive, 0)
        add_chunk(i * OWN_CHUNK, OWN_CHUNK, pairs, held, xh, xl, part)
        return need

    ready = lax.fori_loop(0, (count + OWN_CHUNK - 1) // OWN_CHUNK, chunk, jnp.int32(0))
    lax.fori_loop(ready, NBD, arrive, 0)


def apply_own(pairs, own, tiles):
    vmem = pl.BlockSpec(memory_space=pltpu.VMEM)
    return pl.pallas_call(
        own_kernel,
        out_shape=[pltpu.VMEM((NBD * BS, K), F32), pltpu.VMEM((NBD * TPR, BS, BS), F32)],
        in_specs=[pl.BlockSpec(memory_space=pltpu.SMEM), vmem, pl.BlockSpec(memory_space=pltpu.HBM)],
        out_specs=[vmem] * 2,
        scratch_shapes=[
            pltpu.VMEM(((NBD + 1) * BS, K), BF16),
            pltpu.VMEM(((NBD + 1) * BS, K), BF16),
            pltpu.SemaphoreType.DMA((NBD,)),
        ],
        compiler_params=pltpu.CompilerParams(vmem_limit_bytes=8 * MB),
        cost_estimate=pl.CostEstimate(flops=4 * 10**9, bytes_accessed=25 * MB, transcendentals=0),
        name="apply_own",
    )(pairs, on_vmem(own), pltpu.with_memory_space_constraint(tiles, pltpu.HBM))


def gram_pack(high, low):
    tn = lambda a, b: lax.dot_general(a, b, (((0,), (0,)), ((), ())), preferred_element_type=F32)
    main = tn(high, high)
    cross = tn(high, low)
    gram = main + cross + cross.T
    i = lax.broadcasted_iota(jnp.int32, (BS, BS), 0)
    j = lax.broadcasted_iota(jnp.int32, (BS, BS), 1)
    first, second = gram[:BS, :BS], gram[BS:, BS:]
    diagonal = jnp.sum(jnp.where(i == j, second, 0.0), axis=0, keepdims=True)
    tail = jnp.broadcast_to(diagonal, (2 * HALF - 2 * BS, BS))
    return jnp.concatenate([jnp.where(i <= j, first, second), gram[:BS, BS:], tail], axis=0)


def ghost_kernel(pairs, _, held, px_odd, py_even, px_even, py_odd, total, high, low, gram, xh, xl, xv, ah, al, sems, out_sems):
    arrivals = [pltpu.make_async_copy(g, xv.at[e], sems.at[e]) for e, g in enumerate((px_even, px_odd, py_even, py_odd))]
    for c in arrivals:
        c.start()
    xh[4 * GMAX * BS :] = jnp.zeros((BS, K), BF16)
    xl[4 * GMAX * BS :] = jnp.zeros((BS, K), BF16)
    for e, c in enumerate(arrivals):
        c.wait()

        def convert(s, _):
            rows = pl.ds(pl.multiple_of((e * GMAX + s) * BS, BS), BS)
            xh[rows], xl[rows] = split(xv[e, s])
            return 0

        lax.fori_loop(0, GMAX, convert, 0)

    def chunk(i, _):
        add_chunk(i * GHOST_CHUNK, GHOST_CHUNK, pairs, held, xh, xl, total)
        return 0

    lax.fori_loop(0, (pairs[0] + GHOST_CHUNK - 1) // GHOST_CHUNK, chunk, 0)

    def finish(row, _):
        rows = pl.ds(pl.multiple_of(row * BS, BS), BS)
        ah[rows], al[rows] = split(total[rows])
        return 0

    lax.fori_loop(0, NBD, finish, 0)
    stores = [pltpu.make_async_copy(a, b, out_sems.at[n]) for n, (a, b) in enumerate(((ah, high), (al, low)))]
    for c in stores:
        c.start()
    gram[...] = gram_pack(ah[...], al[...])
    for c in stores:
        c.wait()


def apply_ghosts(pairs, part, held, ghosts):
    smem = pl.BlockSpec(memory_space=pltpu.SMEM)
    vmem = pl.BlockSpec(memory_space=pltpu.VMEM)
    anywhere = pl.BlockSpec(memory_space=pl.ANY)
    hbm = pl.BlockSpec(memory_space=pltpu.HBM)
    _, ah, al, gram = pl.pallas_call(
        ghost_kernel,
        out_shape=[
            pltpu.VMEM((NBD * BS, K), F32),
            pltpu.HBM((NBD * BS, K), BF16),
            pltpu.HBM((NBD * BS, K), BF16),
            jax.ShapeDtypeStruct((2 * HALF, BS), F32),
        ],
        in_specs=[smem] + [vmem] * 2 + [anywhere] * 4,
        out_specs=[vmem, hbm, hbm, vmem],
        scratch_shapes=[
            pltpu.VMEM(((4 * GMAX + 1) * BS, K), BF16),
            pltpu.VMEM(((4 * GMAX + 1) * BS, K), BF16),
            pltpu.VMEM((4, GMAX, BS, K), F32),
            pltpu.VMEM((NBD * BS, K), BF16),
            pltpu.VMEM((NBD * BS, K), BF16),
            pltpu.SemaphoreType.DMA((4,)),
            pltpu.SemaphoreType.DMA((2,)),
        ],
        input_output_aliases={1: 0},
        compiler_params=pltpu.CompilerParams(vmem_limit_bytes=12 * MB),
        cost_estimate=pl.CostEstimate(flops=3 * 10**9, bytes_accessed=25 * MB, transcendentals=0),
        name="apply_ghosts",
    )(pairs, on_vmem(part), on_vmem(held), *ghosts)
    return ah, al, gram


def exact(a, b, ca=1, cb=0):
    return lax.dot_general(
        a, b, (((ca,), (cb,)), ((), ())), precision=lax.Precision.HIGHEST, preferred_element_type=F32
    )


def spread(x):
    return jnp.broadcast_to(x, (8, BS))


def tree_sum(terms):
    while len(terms) > 1:
        pairs = [terms[i] + terms[i + 1] for i in range(0, len(terms) - 1, 2)]
        terms = pairs + terms[len(terms) - len(terms) % 2 :]
    return terms[0]


def eliminate(columns):
    groups, wide = BS // 8, range(len(columns))
    state = [[c[8 * g : 8 * g + 8] for c in columns] for g in range(groups)]
    outs = [[] for _ in columns]
    place = lax.broadcasted_iota(jnp.int32, (8, BS), 0)
    for at in range(groups):
        near = range(at + 1, min(groups, at + 1 + NEAR))
        first = {g: [spread(state[g][0][:, 8 * at + k : 8 * at + k + 1]) for k in range(8)] for g in (at, *near)}
        a = {(i, j): spread(first[at][j][i : i + 1]) for i in range(8) for j in range(i, 8)}
        w = [[spread(state[at][c][k : k + 1]) for c in wide] for k in range(8)]
        inverse, lower = [], {}
        for k in range(8):
            inverse.append(1.0 / a[k, k])
            for i in range(k + 1, 8):
                m = lower[i, k] = a[k, i] * inverse[k]
                for j in range(i, 8):
                    a[i, j] = a[i, j] - m * a[k, j]
                for c in wide:
                    w[i][c] = w[i][c] - m * w[k][c]
        for k in range(8):
            scale = lax.rsqrt(a[k, k])
            for c in wide:
                outs[c].append((w[k][c] * scale)[:1])
        if at + 1 == groups:
            break
        q = [[w[k][c] * inverse[k] for c in wide] for k in range(8)]
        for k in range(6, -1, -1):
            for m in range(k + 1, 8):
                for c in wide:
                    q[k][c] = q[k][c] - lower[m, k] * q[m][c]
        for g in near:
            for c in wide:
                state[g][c] = state[g][c] - tree_sum([first[g][k] * q[k][c] for k in range(8)])
        far = at + 1 + NEAR
        if far < groups:
            rows = []
            for c in wide:
                block = q[0][c]
                for k in range(1, 8):
                    block = jnp.where(place == k, q[k][c], block)
                rows.append(block)
            parts = [jnp.concatenate(rows, axis=1)]
            if at:
                parts.insert(0, jnp.zeros((8 * at, BS * len(columns)), F32))
            parts.append(jnp.zeros((BS - 8 * at - 8, BS * len(columns)), F32))
            update = exact(
                jnp.concatenate([state[g][0] for g in range(far, groups)], axis=0),
                jnp.concatenate(parts, axis=0),
            )
            for n, g in enumerate(range(far, groups)):
                for c in wide:
                    state[g][c] = state[g][c] - update[8 * n : 8 * n + 8, c * BS : c * BS + BS]
    return [jnp.concatenate(rows, axis=0) for rows in outs]


def factor(low, high):
    packed = jnp.concatenate([low, high], axis=0) * (1.0 / NROWS)
    mixed, corner, tail = packed[:BS], packed[BS : 2 * BS], packed[2 * BS : 2 * BS + 1]
    i = lax.broadcasted_iota(jnp.int32, (BS, BS), 0)
    j = lax.broadcasted_iota(jnp.int32, (BS, BS), 1)
    unit = jnp.where(i == j, 1.0, 0.0).astype(F32)
    turned = mixed.T
    first = jnp.where(i <= j, mixed, turned)
    second = jnp.where(i > j, mixed, jnp.where(i < j, turned, tail))
    r11, r12, x11 = eliminate([first, corner, unit])
    x11 = jnp.where(i >= j, x11, 0.0)
    r22, x22 = eliminate([second - exact(r12, r12, 0, 0), unit])
    x22 = jnp.where(i >= j, x22, 0.0)
    x21 = -exact(x22, exact(r12, x11, 0, 0))
    r11, r22 = jnp.where(i <= j, r11, 0.0), jnp.where(i <= j, r22, 0.0)
    zero = jnp.zeros((BS, BS), F32)
    upper = jnp.concatenate(
        [jnp.concatenate([r11, r12], axis=1), jnp.concatenate([zero, r22], axis=1)], axis=0
    )
    lower = jnp.concatenate(
        [jnp.concatenate([x11, zero], axis=1), jnp.concatenate([x21, x22], axis=1)], axis=0
    )
    return upper, lower


def basis_kernel(low, high, rows_high, rows_low, basis, upper, wh, wl, ah, al, staged, in_sems, sems):
    pieces = NBD * BS // STORE

    def piece(n):
        return pl.ds(pl.multiple_of(n * STORE, STORE), STORE)

    def load(n):
        rows = piece(n)
        return [
            pltpu.make_async_copy(a.at[rows], b.at[rows], in_sems.at[k, n])
            for k, (a, b) in enumerate(((rows_high, ah), (rows_low, al)))
        ]

    def store(n):
        return pltpu.make_async_copy(staged.at[piece(n)], basis.at[piece(n)], sems.at[n])

    def begin(n, _):
        for c in load(n):
            c.start()
        return 0

    lax.fori_loop(0, pieces, begin, 0)
    r, x = factor(low[...], high[...])
    upper[...] = r
    wh[...], wl[...] = split(x.T)

    def multiply(n, _):
        for c in load(n):
            c.wait()
        rows = piece(n)
        h, l = ah[rows], al[rows]
        staged[rows] = dot(h, wh[...]) + dot(l, wh[...]) + dot(h, wl[...])
        store(n).start()
        return 0

    lax.fori_loop(0, pieces, multiply, 0)
    for n in range(pieces):
        store(n).wait()


def orthonormalize(low, high, ah, al):
    vmem = pl.BlockSpec(memory_space=pltpu.VMEM)
    hbm = pl.BlockSpec(memory_space=pltpu.HBM)
    return pl.pallas_call(
        basis_kernel,
        out_shape=[
            jax.ShapeDtypeStruct((NBD * BS, K), F32),
            jax.ShapeDtypeStruct((K, K), F32),
        ],
        in_specs=[vmem] * 2 + [hbm] * 2,
        out_specs=[hbm, vmem],
        scratch_shapes=[
            pltpu.VMEM((K, K), BF16),
            pltpu.VMEM((K, K), BF16),
            pltpu.VMEM((NBD * BS, K), BF16),
            pltpu.VMEM((NBD * BS, K), BF16),
            pltpu.VMEM((NBD * BS, K), F32),
            pltpu.SemaphoreType.DMA((2, NBD * BS // STORE)),
            pltpu.SemaphoreType.DMA((NBD * BS // STORE,)),
        ],
        compiler_params=pltpu.CompilerParams(vmem_limit_bytes=12 * MB),
        cost_estimate=pl.CostEstimate(flops=10**9, bytes_accessed=7 * MB, transcendentals=0),
        name="factor_and_basis",
    )(low, high, *[pltpu.with_memory_space_constraint(a, pltpu.HBM) for a in (ah, al)])


def body(block_vectors, stiff_tiles, col_index, send_lists, send_counts, part_blocks):
    parity = jnp.stack([lax.axis_index("px") % 2, lax.axis_index("py") % 2]).astype(jnp.int32)
    tiles = stiff_tiles.reshape(NBD * TPR, BS, BS)
    (px_odd, px_even, py_odd, py_even), (own_pairs, ghost_pairs) = prepare(
        parity, send_lists, send_counts, col_index.T, part_blocks, block_vectors
    )
    px_odd = swapped(px_odd, "px", True)
    py_even = swapped(py_even, "py", False)
    px_even = swapped(px_even, "px", False)
    py_odd = swapped(py_odd, "py", True)
    part, held = apply_own(own_pairs, block_vectors, tiles)
    ah, al, gram = apply_ghosts(ghost_pairs, part, held, [px_odd, py_even, px_even, py_odd])
    low, high = sum_everywhere(gram)
    return tuple(orthonormalize(low, high, ah, al))


def solution(mesh):
    placed = (
        P(AXES, None),
        P(AXES, None, None, None),
        P(AXES, None),
        P(AXES, None, None),
        P(AXES, None),
        P(AXES),
    )
    return jax.shard_map(body, mesh=mesh, in_specs=placed, out_specs=(P(AXES, None), P()), check_vma=False)
```

```python
import functools
import itertools

import jax
import jax.numpy as jnp
from jax import lax
from jax.experimental import pallas as pl
from jax.experimental.pallas import tpu as pltpu
from jax.sharding import PartitionSpec as P

AXES = ("px", "py")
SIDE = 4
BS = 128
K = 256
NBD = 24
TPR = 12
GMAX = 4
NROWS = 393216
HALF = 136
F32 = jnp.float32
BF16 = jnp.bfloat16
MB = 1 << 20
OWN_CHUNK = 8
GHOST_CHUNK = 12
LIST_AT = 8
LIST_SIZE = LIST_AT + NBD * TPR + 2 * NBD + 32
TILE_SHIFT = 6
ROW_SHIFT = 16
TILE_UNIT = 1 << TILE_SHIFT
ROW_UNIT = 1 << ROW_SHIFT
AHEAD = 9
NEAR = 2
STORE = 1024


def device_at(x, y, z, core):
    return (y * SIDE + x) * 8 + z * 2 + core


def route(move):
    places = itertools.product(range(SIDE), range(SIDE), range(SIDE), range(2))
    return [(device_at(*p), device_at(*move(*p))) for p in places]


def pair_route(dim, odd):
    def move(x, y, z, core):
        at = [x, y, z]
        v = at[dim]
        if odd:
            at[dim] = (v - 1) % SIDE if v % 2 == 0 else (v + 1) % SIDE
        else:
            at[dim] = v ^ 1
        return (*at, core)

    return route(move)


CORE_ROUTE = route(lambda x, y, z, core: (x, y, z, 1 - core))


def far_route(dim):
    def move(x, y, z, core):
        at = [x, y, z]
        at[dim] ^= 2
        return (*at, core)

    return route(move)


def swapped(block, axis, odd):
    n = lax.axis_size(axis)
    pairs = [(i, i + 1) for i in range(1 if odd else 0, n - 1, 2)]
    return lax.ppermute(block, axis, pairs + [(j, i) for i, j in pairs])


def sum_everywhere(packed):
    core = lax.axis_index("py") % 2
    mine = lax.dynamic_slice_in_dim(packed, core * HALF, HALF, 0)
    other = lax.dynamic_slice_in_dim(packed, (1 - core) * HALF, HALF, 0)
    total = mine + lax.ppermute(other, AXES, CORE_ROUTE)
    for dim in range(3):
        routes = (pair_route(dim, False), pair_route(dim, True), far_route(dim))
        near, wrap, far = [lax.ppermute(total, AXES, r) for r in routes]
        total = (total + near) + (wrap + far)
    theirs = lax.ppermute(total, AXES, CORE_ROUTE)
    low = jnp.where(core == 0, total, theirs)
    high = jnp.where(core == 0, theirs, total)
    return low, high


def on_vmem(x):
    return pltpu.with_memory_space_constraint(x, pltpu.VMEM)


def split(x):
    high = x.astype(BF16)
    return high, (x - high.astype(F32)).astype(BF16)


def dot(a, b):
    return lax.dot_general(a, b, (((1,), (0,)), ((), ())), preferred_element_type=F32)


def pair_lists(parity, cols, live, own_list, ghost_list):
    turn_px, turn_py = GMAX * (1 - parity[0]), GMAX * (1 - parity[1])

    def row_pairs(row, counts):
        own_n, ghost_n = counts
        base = row * (ROW_UNIT + TPR * TILE_UNIT)
        for t in range(TPR):
            c = cols[t, row]
            ghost = jnp.where(c >= NBD, 1, 0)
            g = c - NBD
            entry = base + t * TILE_UNIT
            own_list[LIST_AT + own_n] = entry + c
            ghost_list[LIST_AT + ghost_n] = entry + (g ^ jnp.where(g < 2 * GMAX, turn_px, turn_py))
            own_n, ghost_n = own_n + 1 - ghost, ghost_n + ghost
        own_list[LIST_AT + own_n] = NBD
        ghost_list[LIST_AT + ghost_n] = 4 * GMAX
        return own_n + (own_n & 1), ghost_n + (ghost_n & 1)

    zero = jnp.int32(0)
    ends = lax.fori_loop(0, live[0], row_pairs, (zero, zero))
    for out, n, blank, chunk in (
        (own_list, ends[0], NBD, OWN_CHUNK),
        (ghost_list, ends[1], 4 * GMAX, GHOST_CHUNK),
    ):
        for k in range(2 * chunk):
            out[LIST_AT + n + k] = blank
        out[0] = n >> 1


def prepare_kernel(parity, lists_in, counts_in, own, *refs):
    outs, (lists, counts, held) = refs[:4], refs[4:7]
    small_sems, in_sems, out_sems = refs[7:]
    small = [
        pltpu.make_async_copy(a, b, small_sems.at[n])
        for n, (a, b) in enumerate(((lists_in, lists), (counts_in, counts)))
    ]
    for c in small:
        c.start()
    odd_px, odd_py = parity[0], parity[1]
    directions = (1 - odd_px, odd_px, 3 - odd_py, 2 + odd_py)

    def fetch(n, s):
        block = lists[0, directions[n], s]
        rows = pl.ds(pl.multiple_of(block * BS, BS), BS)
        return pltpu.make_async_copy(own.at[rows], held.at[n, s], in_sems.at[n, s])

    def store(n, s):
        return pltpu.make_async_copy(held.at[n, s], outs[n].at[s], out_sems.at[n, s])

    small[0].wait()
    for n in range(4):
        for s in range(GMAX):
            fetch(n, s).start()
    for c in small[1:]:
        c.wait()
    for n in range(4):
        for s in range(GMAX):
            fetch(n, s).wait()

            @pl.when(s >= counts[0, directions[n]])
            def _():
                held[n, s] = jnp.zeros((BS, K), F32)

            store(n, s).start()
    for n in range(4):
        for s in range(GMAX):
            store(n, s).wait()


def prepare(parity, lists, counts, own):
    smem = pl.BlockSpec(memory_space=pltpu.SMEM)
    hbm = pl.BlockSpec(memory_space=pltpu.HBM)
    anywhere = pl.BlockSpec(memory_space=pl.ANY)
    arrays = (lists, counts, own)
    return pl.pallas_call(
        prepare_kernel,
        out_shape=[jax.ShapeDtypeStruct((GMAX, BS, K), F32)] * 4,
        in_specs=[smem] + [hbm] * 3,
        out_specs=[anywhere] * 4,
        scratch_shapes=[
            *[pltpu.SMEM(a.shape, jnp.int32) for a in arrays[:2]],
            pltpu.VMEM((4, GMAX, BS, K), F32),
            pltpu.SemaphoreType.DMA((2,)),
            pltpu.SemaphoreType.DMA((4, GMAX)),
            pltpu.SemaphoreType.DMA((4, GMAX)),
        ],
        compiler_params=pltpu.CompilerParams(vmem_limit_bytes=4 * MB),
        cost_estimate=pl.CostEstimate(flops=0, bytes_accessed=4 * MB, transcendentals=0),
        name="prepare",
    )(parity, *[pltpu.with_memory_space_constraint(a, pltpu.HBM) for a in arrays])


def add_chunk(start, size, pairs, tiles, xh, xl, acc):
    for k in range(size):
        first = pairs[LIST_AT + 2 * (start + k)]
        second = pairs[LIST_AT + 2 * (start + k) + 1]
        t0, t1 = (first >> TILE_SHIFT) & 1023, (second >> TILE_SHIFT) & 1023
        c0, c1 = first & 63, second & 63
        th, tl = split(jnp.concatenate([tiles[t0], tiles[t1]], axis=1))
        r0 = pl.ds(pl.multiple_of(c0 * BS, BS), BS)
        r1 = pl.ds(pl.multiple_of(c1 * BS, BS), BS)
        bh = jnp.concatenate([xh[r0], xh[r1]], axis=0)
        bl = jnp.concatenate([xl[r0], xl[r1]], axis=0)
        at = pl.ds(pl.multiple_of((first >> ROW_SHIFT) * BS, BS), BS)
        acc[at] += dot(th, bh) + dot(tl, bh) + dot(th, bl)


def own_kernel(parity, cols, live, own, tiles, part, held, ghost_pairs, xh, xl, pairs, sems):
    def fetch(row):
        rows = pl.ds(row * TPR, TPR)
        return pltpu.make_async_copy(tiles.at[rows], held.at[rows], sems.at[row])

    for row in range(AHEAD):
        fetch(row).start()
    pair_lists(parity, cols, live, pairs, ghost_pairs)
    xh[NBD * BS :] = jnp.zeros((BS, K), BF16)
    xl[NBD * BS :] = jnp.zeros((BS, K), BF16)

    def convert(b, _):
        rows = pl.ds(pl.multiple_of(b * BS, BS), BS)
        xh[rows], xl[rows] = split(own[rows])
        part[rows] = jnp.zeros((BS, K), F32)
        return 0

    lax.fori_loop(0, NBD, convert, 0)

    def arrive(row, _):
        fetch(row).wait()

        @pl.when(row + AHEAD < NBD)
        def _():
            fetch(row + AHEAD).start()

        return 0

    count = pairs[0]

    def chunk(i, ready):
        last = jnp.minimum(i * OWN_CHUNK + OWN_CHUNK, count) - 1
        need = jnp.maximum((pairs[LIST_AT + 2 * last] >> ROW_SHIFT) + 1, ready)
        lax.fori_loop(ready, need, arrive, 0)
        add_chunk(i * OWN_CHUNK, OWN_CHUNK, pairs, held, xh, xl, part)
        return need

    ready = lax.fori_loop(0, (count + OWN_CHUNK - 1) // OWN_CHUNK, chunk, jnp.int32(0))
    lax.fori_loop(ready, NBD, arrive, 0)


def apply_own(parity, cols, live, own, tiles):
    smem = pl.BlockSpec(memory_space=pltpu.SMEM)
    vmem = pl.BlockSpec(memory_space=pltpu.VMEM)
    return pl.pallas_call(
        own_kernel,
        out_shape=[
            pltpu.VMEM((NBD * BS, K), F32),
            pltpu.VMEM((NBD * TPR, BS, BS), F32),
            jax.ShapeDtypeStruct((LIST_SIZE,), jnp.int32),
        ],
        in_specs=[smem] * 3 + [vmem, pl.BlockSpec(memory_space=pltpu.HBM)],
        out_specs=[vmem, vmem, smem],
        scratch_shapes=[
            pltpu.VMEM(((NBD + 1) * BS, K), BF16),
            pltpu.VMEM(((NBD + 1) * BS, K), BF16),
            pltpu.SMEM((LIST_SIZE,), jnp.int32),
            pltpu.SemaphoreType.DMA((NBD,)),
        ],
        compiler_params=pltpu.CompilerParams(vmem_limit_bytes=8 * MB),
        cost_estimate=pl.CostEstimate(flops=4 * 10**9, bytes_accessed=25 * MB, transcendentals=0),
        name="apply_own",
    )(parity, cols, live, on_vmem(own), pltpu.with_memory_space_constraint(tiles, pltpu.HBM))


def gram_pack(high, low):
    tn = lambda a, b: lax.dot_general(a, b, (((0,), (0,)), ((), ())), preferred_element_type=F32)
    main = tn(high, high)
    cross = tn(high, low)
    gram = main + cross + cross.T
    i = lax.broadcasted_iota(jnp.int32, (BS, BS), 0)
    j = lax.broadcasted_iota(jnp.int32, (BS, BS), 1)
    first, second = gram[:BS, :BS], gram[BS:, BS:]
    diagonal = jnp.sum(jnp.where(i == j, second, 0.0), axis=0, keepdims=True)
    tail = jnp.broadcast_to(diagonal, (2 * HALF - 2 * BS, BS))
    return jnp.concatenate([jnp.where(i <= j, first, second), gram[:BS, BS:], tail], axis=0)


def ghost_kernel(pairs, _, held, g0, g1, g2, g3, total, high, low, gram, xh, xl, xv, ah, al, sems, out_sems):
    arrivals = [pltpu.make_async_copy(g, xv.at[e], sems.at[e]) for e, g in enumerate((g0, g1, g2, g3))]
    for c in arrivals:
        c.start()
    xh[4 * GMAX * BS :] = jnp.zeros((BS, K), BF16)
    xl[4 * GMAX * BS :] = jnp.zeros((BS, K), BF16)
    for e, c in enumerate(arrivals):
        c.wait()

        def convert(s, _):
            rows = pl.ds(pl.multiple_of((e * GMAX + s) * BS, BS), BS)
            xh[rows], xl[rows] = split(xv[e, s])
            return 0

        lax.fori_loop(0, GMAX, convert, 0)

    def chunk(i, _):
        add_chunk(i * GHOST_CHUNK, GHOST_CHUNK, pairs, held, xh, xl, total)
        return 0

    lax.fori_loop(0, (pairs[0] + GHOST_CHUNK - 1) // GHOST_CHUNK, chunk, 0)

    def finish(row, _):
        rows = pl.ds(pl.multiple_of(row * BS, BS), BS)
        ah[rows], al[rows] = split(total[rows])
        return 0

    lax.fori_loop(0, NBD, finish, 0)
    stores = [pltpu.make_async_copy(a, b, out_sems.at[n]) for n, (a, b) in enumerate(((ah, high), (al, low)))]
    for c in stores:
        c.start()
    gram[...] = gram_pack(ah[...], al[...])
    for c in stores:
        c.wait()


def apply_ghosts(pairs, part, held, ghosts):
    smem = pl.BlockSpec(memory_space=pltpu.SMEM)
    vmem = pl.BlockSpec(memory_space=pltpu.VMEM)
    anywhere = pl.BlockSpec(memory_space=pl.ANY)
    hbm = pl.BlockSpec(memory_space=pltpu.HBM)
    _, ah, al, gram = pl.pallas_call(
        ghost_kernel,
        out_shape=[
            pltpu.VMEM((NBD * BS, K), F32),
            pltpu.HBM((NBD * BS, K), BF16),
            pltpu.HBM((NBD * BS, K), BF16),
            jax.ShapeDtypeStruct((2 * HALF, BS), F32),
        ],
        in_specs=[smem] + [vmem] * 2 + [anywhere] * 4,
        out_specs=[vmem, hbm, hbm, vmem],
        scratch_shapes=[
            pltpu.VMEM(((4 * GMAX + 1) * BS, K), BF16),
            pltpu.VMEM(((4 * GMAX + 1) * BS, K), BF16),
            pltpu.VMEM((4, GMAX, BS, K), F32),
            pltpu.VMEM((NBD * BS, K), BF16),
            pltpu.VMEM((NBD * BS, K), BF16),
            pltpu.SemaphoreType.DMA((4,)),
            pltpu.SemaphoreType.DMA((2,)),
        ],
        input_output_aliases={1: 0},
        compiler_params=pltpu.CompilerParams(vmem_limit_bytes=12 * MB),
        cost_estimate=pl.CostEstimate(flops=3 * 10**9, bytes_accessed=25 * MB, transcendentals=0),
        name="apply_ghosts",
    )(pairs, on_vmem(part), on_vmem(held), *ghosts)
    return ah, al, gram


def exact(a, b, ca=1, cb=0):
    return lax.dot_general(
        a, b, (((ca,), (cb,)), ((), ())), precision=lax.Precision.HIGHEST, preferred_element_type=F32
    )


def spread(x):
    return jnp.broadcast_to(x, (8, BS))


def tree_sum(terms):
    while len(terms) > 1:
        pairs = [terms[i] + terms[i + 1] for i in range(0, len(terms) - 1, 2)]
        terms = pairs + terms[len(terms) - len(terms) % 2 :]
    return terms[0]


def eliminate(columns):
    groups, wide = BS // 8, range(len(columns))
    state = [[c[8 * g : 8 * g + 8] for c in columns] for g in range(groups)]
    outs = [[] for _ in columns]
    place = lax.broadcasted_iota(jnp.int32, (8, BS), 0)
    for at in range(groups):
        near = range(at + 1, min(groups, at + 1 + NEAR))
        first = {g: [spread(state[g][0][:, 8 * at + k : 8 * at + k + 1]) for k in range(8)] for g in (at, *near)}
        a = {(i, j): spread(first[at][j][i : i + 1]) for i in range(8) for j in range(i, 8)}
        w = [[spread(state[at][c][k : k + 1]) for c in wide] for k in range(8)]
        inverse, lower = [], {}
        for k in range(8):
            inverse.append(1.0 / a[k, k])
            for i in range(k + 1, 8):
                m = lower[i, k] = a[k, i] * inverse[k]
                for j in range(i, 8):
                    a[i, j] = a[i, j] - m * a[k, j]
                for c in wide:
                    w[i][c] = w[i][c] - m * w[k][c]
        for k in range(8):
            scale = lax.rsqrt(a[k, k])
            for c in wide:
                outs[c].append((w[k][c] * scale)[:1])
        if at + 1 == groups:
            break
        q = [[w[k][c] * inverse[k] for c in wide] for k in range(8)]
        for k in range(6, -1, -1):
            for m in range(k + 1, 8):
                for c in wide:
                    q[k][c] = q[k][c] - lower[m, k] * q[m][c]
        for g in near:
            for c in wide:
                state[g][c] = state[g][c] - tree_sum([first[g][k] * q[k][c] for k in range(8)])
        far = at + 1 + NEAR
        if far < groups:
            rows = []
            for c in wide:
                block = q[0][c]
                for k in range(1, 8):
                    block = jnp.where(place == k, q[k][c], block)
                rows.append(block)
            parts = [jnp.concatenate(rows, axis=1)]
            if at:
                parts.insert(0, jnp.zeros((8 * at, BS * len(columns)), F32))
            parts.append(jnp.zeros((BS - 8 * at - 8, BS * len(columns)), F32))
            update = exact(
                jnp.concatenate([state[g][0] for g in range(far, groups)], axis=0),
                jnp.concatenate(parts, axis=0),
            )
            for n, g in enumerate(range(far, groups)):
                for c in wide:
                    state[g][c] = state[g][c] - update[8 * n : 8 * n + 8, c * BS : c * BS + BS]
    return [jnp.concatenate(rows, axis=0) for rows in outs]


def factor(low, high):
    packed = jnp.concatenate([low, high], axis=0) * (1.0 / NROWS)
    mixed, corner, tail = packed[:BS], packed[BS : 2 * BS], packed[2 * BS : 2 * BS + 1]
    i = lax.broadcasted_iota(jnp.int32, (BS, BS), 0)
    j = lax.broadcasted_iota(jnp.int32, (BS, BS), 1)
    unit = jnp.where(i == j, 1.0, 0.0).astype(F32)
    turned = mixed.T
    first = jnp.where(i <= j, mixed, turned)
    second = jnp.where(i > j, mixed, jnp.where(i < j, turned, tail))
    r11, r12, x11 = eliminate([first, corner, unit])
    x11 = jnp.where(i >= j, x11, 0.0)
    r22, x22 = eliminate([second - exact(r12, r12, 0, 0), unit])
    x22 = jnp.where(i >= j, x22, 0.0)
    x21 = -exact(x22, exact(r12, x11, 0, 0))
    r11, r22 = jnp.where(i <= j, r11, 0.0), jnp.where(i <= j, r22, 0.0)
    zero = jnp.zeros((BS, BS), F32)
    upper = jnp.concatenate(
        [jnp.concatenate([r11, r12], axis=1), jnp.concatenate([zero, r22], axis=1)], axis=0
    )
    lower = jnp.concatenate(
        [jnp.concatenate([x11, zero], axis=1), jnp.concatenate([x21, x22], axis=1)], axis=0
    )
    return upper, lower


def basis_kernel(low, high, rows_high, rows_low, basis, upper, wh, wl, ah, al, staged, in_sems, sems):
    pieces = NBD * BS // STORE

    def piece(n):
        return pl.ds(pl.multiple_of(n * STORE, STORE), STORE)

    def load(n):
        rows = piece(n)
        return [
            pltpu.make_async_copy(a.at[rows], b.at[rows], in_sems.at[k, n])
            for k, (a, b) in enumerate(((rows_high, ah), (rows_low, al)))
        ]

    def store(n):
        return pltpu.make_async_copy(staged.at[piece(n)], basis.at[piece(n)], sems.at[n])

    def begin(n, _):
        for c in load(n):
            c.start()
        return 0

    lax.fori_loop(0, pieces, begin, 0)
    r, x = factor(low[...], high[...])
    upper[...] = r
    wh[...], wl[...] = split(x.T)

    def multiply(n, _):
        for c in load(n):
            c.wait()
        rows = piece(n)
        h, l = ah[rows], al[rows]
        staged[rows] = dot(h, wh[...]) + dot(l, wh[...]) + dot(h, wl[...])
        store(n).start()
        return 0

    lax.fori_loop(0, pieces, multiply, 0)
    for n in range(pieces):
        store(n).wait()


def orthonormalize(low, high, ah, al):
    vmem = pl.BlockSpec(memory_space=pltpu.VMEM)
    hbm = pl.BlockSpec(memory_space=pltpu.HBM)
    return pl.pallas_call(
        basis_kernel,
        out_shape=[
            jax.ShapeDtypeStruct((NBD * BS, K), F32),
            jax.ShapeDtypeStruct((K, K), F32),
        ],
        in_specs=[vmem] * 2 + [hbm] * 2,
        out_specs=[hbm, vmem],
        scratch_shapes=[
            pltpu.VMEM((K, K), BF16),
            pltpu.VMEM((K, K), BF16),
            pltpu.VMEM((NBD * BS, K), BF16),
            pltpu.VMEM((NBD * BS, K), BF16),
            pltpu.VMEM((NBD * BS, K), F32),
            pltpu.SemaphoreType.DMA((2, NBD * BS // STORE)),
            pltpu.SemaphoreType.DMA((NBD * BS // STORE,)),
        ],
        compiler_params=pltpu.CompilerParams(vmem_limit_bytes=12 * MB),
        cost_estimate=pl.CostEstimate(flops=10**9, bytes_accessed=7 * MB, transcendentals=0),
        name="factor_and_basis",
    )(low, high, *[pltpu.with_memory_space_constraint(a, pltpu.HBM) for a in (ah, al)])


def body(block_vectors, stiff_tiles, col_index, send_lists, send_counts, part_blocks):
    parity = jnp.stack([lax.axis_index("px") % 2, lax.axis_index("py") % 2]).astype(jnp.int32)
    tiles = stiff_tiles.reshape(NBD * TPR, BS, BS)
    px_odd, px_even, py_odd, py_even = prepare(parity, send_lists, send_counts, block_vectors)
    px_odd = swapped(px_odd, "px", True)
    py_even = swapped(py_even, "py", False)
    px_even = swapped(px_even, "px", False)
    py_odd = swapped(py_odd, "py", True)
    part, held, ghost_pairs = apply_own(parity, col_index.T, part_blocks, block_vectors, tiles)
    ah, al, gram = apply_ghosts(ghost_pairs, part, held, [px_even, px_odd, py_even, py_odd])
    low, high = sum_everywhere(gram)
    return tuple(orthonormalize(low, high, ah, al))


def solution(mesh):
    placed = (
        P(AXES, None),
        P(AXES, None, None, None),
        P(AXES, None),
        P(AXES, None, None),
        P(AXES, None),
        P(AXES),
    )
    return jax.shard_map(body, mesh=mesh, in_specs=placed, out_specs=(P(AXES, None), P()), check_vma=False)
```
